512 devices in a mesh: tok: 32 (over z_hi, x, core), word: 16 (over y, z_lo).
Axes of the slice: x: 4, y: 4, z: 16 (z_hi: 4, z_lo: 4; z = z_hi * 4 + z_lo), core: 2. Of those that a mesh axis runs over, the one named last changes fastest.
Arguments:
- char_ids: int32 [24, 53248], P(None, 'tok'), may hold values from 0 to 255
- char_table: bfloat16 [256, 16], replicated, may hold values from -6 to 6
- conv_weight: bfloat16 [112, 2048], P(None, 'word'), may hold values from -0.75 to 0.75
- conv_bias: float32 [2048], P('word'), may hold values from -2 to 0
- highway_hid: bfloat16 [2048, 2048], P(None, 'word'), may hold values from -0.125 to 0.125
- highway_gate: bfloat16 [2048, 2048], P(None, 'word'), may hold values from -0.125 to 0.125
- hid_bias: float32 [2048], P('word'), may hold values from -0.5 to 0.5
- gate_bias: float32 [2048], P('word'), may hold values from -2 to 0
- proj_weight: bfloat16 [2048, 1024], P('word'), may hold values from -0.125 to 0.125
- hidden: bfloat16 [8192, 1024], P('tok'), may hold values from -16 to 16
- targets: int32 [8192], replicated, may hold values from 0 to 53247
- counts: int32 [32], replicated, may hold values from 0 to 256, as said below
Outputs:
- embeddings: bfloat16 [53248, 1024], P(('tok', 'word'))
- logprob: float32 [8192], P('tok')
The draws below stay inside these ranges and needn't reach their ends.
Inputs may be any that keep to these rules, and one draw needn't show every extreme that they name: For every s below 16, counts[s] + counts[s + 16] = 256; some shard holds 256 rows.
All inputs are finite; a program needn't handle non-finite values.
Results may differ from the reference program's by a relative error of at most 0.022.
Values may be sent and summed in bfloat16 or wider, within the bound.
A program may use at most 64 MiB of HBM per device.

```python
import math
import jax
import jax.numpy as jnp
import numpy as np
from jax import lax

CHARS = 256
CHAR_DIM = 16
KMAX = 7
CHAR_LEN = 24
FILTERS = 2048
D = 1024
TOK_DEV = 256
WORDS = 53248
ROW_WORDS = 1664
FILT_DEV = 128
TOKENS = 8192
TOK_SHARDS = 32
N_TOK = 32
N_WORD = 16


def draw_counts(key, part):
    half_shards = TOK_SHARDS // 2
    lower = jax.random.randint(jax.random.fold_in(key, 11), (half_shards,), 0, TOK_DEV + 1)
    chosen = jax.random.randint(jax.random.fold_in(key, 12), (), 0, half_shards)
    lower = jnp.where(jnp.arange(half_shards) == chosen, TOK_DEV, lower)
    return jnp.concatenate([lower, TOK_DEV - lower]).astype(jnp.int32)


def draw_hidden(key, part):
    value_key = jax.random.fold_in(key, 21)
    values = 0.2 * jax.random.truncated_normal(value_key, -6.0, 6.0, (TOKENS, D), jnp.float32)
    loud = jax.random.randint(jax.random.fold_in(key, 23), (TOKENS, 1), 0, 8) == 0
    sign_bits = jax.random.randint(jax.random.fold_in(key, 25), (TOKENS, D), 0, 2)
    signs = 2.0 * sign_bits.astype(jnp.float32) - 1.0
    level = min(16.0, 96.0 / math.sqrt(D))
    magnitude = jax.random.uniform(jax.random.fold_in(key, 24), (TOKENS, D), jnp.float32, 0.6, 1.0)
    values = jnp.where(loud, signs * magnitude * level, values)
    return values.astype(jnp.bfloat16)


def place_ends(entries, own_key, low, largest):
    extent = entries.shape
    index_at = [jax.random.randint(jax.random.fold_in(own_key, axis), (), 0, extent[axis]) for axis in range(len(extent))]
    entries = entries.at[tuple(index_at)].set(low)
    longest = extent.index(max(extent))
    index_at[longest] = (index_at[longest] + 1) % extent[longest]
    return entries.at[tuple(index_at)].set(largest)


def levels(rng, shape, pieces, least, largest):
    gain, own = 1.0, jax.random.fold_in(rng, 6)
    for axis_at, blocks in pieces:
        draws = jnp.exp(jax.random.uniform(jax.random.fold_in(own, axis_at), (blocks,), jnp.float32, least / len(pieces), largest / len(pieces)))
        gain = gain * jnp.repeat(draws, shape[axis_at] // blocks).reshape([-1 if axis == axis_at else 1 for axis in range(len(shape))])
    return gain


def cumulative_ranks(count, slope):
    loads = [(1 << 20) // math.isqrt(grade ** slope) + 1 for grade in range(1, count + 1)]
    deviation = 1 + sum(loads) // (1 << 30)
    return np.cumsum(np.array([max(1, weight // deviation) for weight in loads]))


def ranked(key, shape, count, slope):
    table = cumulative_ranks(count, slope)
    ticket = jax.random.randint(jax.random.fold_in(key, 1), shape, 0, int(table[count - 1]))
    rank = jnp.searchsorted(jnp.asarray(table, jnp.int32), ticket, side="right")
    return jax.random.permutation(jax.random.fold_in(key, 2), count)[rank].astype(jnp.int32)


def centred(key, shape, width, bound, cuts=(), kind=jnp.bfloat16):
    level = levels(key, shape, cuts, -0.22, 0.18) if cuts else 1.0
    values = jax.random.normal(key, shape, jnp.float32) * width * level
    return jnp.minimum(jnp.maximum(values, -bound), bound).astype(kind)


def setup_inputs(seed: int = 0) -> dict:
    keys = jax.random.split(jax.random.key(seed), 13)
    return {
        "char_ids": place_ends(jax.random.randint(keys[0], (CHAR_LEN, WORDS), 0, CHARS), jax.random.fold_in(keys[0], 1), 0, CHARS - 1).astype(jnp.int32),
        "char_table": centred(keys[1], (CHARS, CHAR_DIM), 1.0, 6.0),
        "conv_weight": centred(keys[2], (KMAX * CHAR_DIM, FILTERS), (CHAR_DIM * 4) ** -0.5, 0.75, ((1, 16),)),
        "conv_bias": jnp.clip(-2.0 + 2.0 * jax.random.uniform(keys[3], (FILTERS,), jnp.float32) ** levels(keys[3], (FILTERS,), ((0, 16),), -0.2, 0.2), -2.0, 0.0),
        "highway_hid": centred(keys[4], (FILTERS, FILTERS), FILTERS ** -0.5, 0.125, ((1, 16),)),
        "highway_gate": centred(keys[5], (FILTERS, FILTERS), FILTERS ** -0.5, 0.125, ((1, 16),)),
        "hid_bias": jnp.clip(jax.random.uniform(keys[6], (FILTERS,), jnp.float32, -0.5, 0.5) * levels(keys[6], (FILTERS,), ((0, 16),), -0.4, 0.0), -0.5, 0.5),
        "gate_bias": jnp.clip(-2.0 + 2.0 * jax.random.uniform(keys[7], (FILTERS,), jnp.float32) ** levels(keys[7], (FILTERS,), ((0, 16),), -0.2, 0.2), -2.0, 0.0),
        "proj_weight": centred(keys[8], (FILTERS, D), FILTERS ** -0.5, 0.125, ((0, 16),)),
        "hidden": draw_hidden(jax.random.fold_in(keys[12], 71), 0),
        "targets": place_ends(ranked(keys[10], (TOKENS,), WORDS, 2), jax.random.fold_in(keys[10], 3), 0, WORDS - 1).astype(jnp.int32),
        "counts": draw_counts(jax.random.fold_in(keys[12], 71), 0),
    }


def filter_mask(first_filter, amount):
    position_row = jnp.arange(KMAX * CHAR_DIM, dtype=jnp.int32) // CHAR_DIM
    filter_index = first_filter + jnp.arange(amount, dtype=jnp.int32)
    filter_width = 1 + (filter_index * KMAX) // FILTERS
    return position_row[:, None] < filter_width[None, :]


def window_rows(char_table, char_block):
    embedded = jnp.take(char_table, char_block.T, axis=0)
    padded = jnp.pad(embedded, ((0, 0), (0, KMAX - 1), (0, 0)))
    return jnp.concatenate([padded[:, offset_k:offset_k + CHAR_LEN, :] for offset_k in range(KMAX)], axis=2)


def reference(char_ids, char_table, conv_weight, conv_bias, highway_hid, highway_gate, hid_bias, gate_bias, proj_weight, hidden, targets, counts):
    masked = conv_weight.astype(jnp.float32) * filter_mask(0, FILTERS).astype(jnp.float32)

    def conv_block(char_block):
        windows = window_rows(char_table, char_block).astype(jnp.float32)
        conv = jnp.einsum("wpc,cf->wpf", windows, masked, precision=lax.Precision.HIGHEST)
        return jnp.tanh(jnp.max(conv, axis=1) + conv_bias).astype(jnp.bfloat16)

    def build_row(row_chars):
        blocks = row_chars.reshape(CHAR_LEN, 8, ROW_WORDS // 8).transpose(1, 0, 2)
        feats = lax.map(conv_block, blocks).reshape(ROW_WORDS, FILTERS)
        hid_in = jnp.dot(feats, highway_hid, preferred_element_type=jnp.float32) + hid_bias
        gate_in = jnp.dot(feats, highway_gate, preferred_element_type=jnp.float32) + gate_bias
        opened = jax.nn.sigmoid(gate_in)
        highway = (opened * jax.nn.relu(hid_in) + (1.0 - opened) * feats.astype(jnp.float32)).astype(jnp.bfloat16)
        grouped = highway.astype(jnp.float32).reshape(ROW_WORDS, N_WORD, FILT_DEV)
        weights = proj_weight.astype(jnp.float32).reshape(N_WORD, FILT_DEV, D)
        parts = jnp.einsum("wgk,gkd->gwd", grouped, weights, precision=lax.Precision.HIGHEST)
        parts = lax.optimization_barrier(parts.astype(jnp.bfloat16)).astype(jnp.float32)
        return jnp.sum(parts, axis=0).astype(jnp.bfloat16)

    row_sets = char_ids.reshape(CHAR_LEN, N_TOK, ROW_WORDS).transpose(1, 0, 2)
    embeddings = lax.map(build_row, row_sets).reshape(WORDS, D)
    embed_cols = embeddings.T

    def shard_logprob(inputs):
        shard_rows, shard_targets, shard_count = inputs
        scores = jnp.dot(shard_rows, embed_cols, preferred_element_type=jnp.float32)
        top_score = jnp.max(scores, axis=1)
        log_total = top_score + jnp.log(jnp.sum(jnp.exp(scores - top_score[:, None]), axis=1))
        picked = jnp.take_along_axis(scores, shard_targets[:, None].astype(jnp.int32), axis=1)[:, 0]
        labelled = jnp.arange(TOK_DEV, dtype=jnp.int32) < shard_count
        return jnp.where(labelled, picked - log_total, jnp.float32(0.0))

    logprob = lax.map(shard_logprob, (hidden.reshape(N_TOK, TOK_DEV, D), targets.reshape(N_TOK, TOK_DEV), counts))
    return embeddings, logprob.reshape(TOKENS)
```

```python
import functools

import jax
import jax.numpy as jnp
from jax import lax
from jax.experimental import pallas as pl
from jax.experimental.pallas import tpu as pltpu
from jax.sharding import PartitionSpec as P

CHAR_DIM = 16
KMAX = 7
CHAR_LEN = 24
FILTERS = 2048
TOK_DEV = 256
ROW_BLOCK = 64
MESH = pl.DeviceIdType.MESH
BF16 = jnp.bfloat16
F32 = jnp.float32

GROUP = 4
OWN = 104
BLOCK = GROUP * OWN
SLICE = 128
WIDE = GROUP * SLICE
PACK = 2560
CHUNK = PACK // 8


lowest_score = -1e30


def dot(a, b):
    return jnp.dot(a, b, preferred_element_type=F32)


def embed_kernel(
    ids_ref, table_ref, conv_ref, cbias_ref, hid_ref, gate_ref, hbias_ref, gbias_ref, proj_ref,
    out_ref,
    weights, convs, biases, tables, chars, shifted, best, feats, highway, parts, arrived,
    send_sem, recv_sem,
):
    tok, word = lax.axis_index("tok"), lax.axis_index("word")
    zhi, x, core = tok // 8, (tok // 2) % 4, tok % 2
    y, zlo = word // 4, word % 4

    def at(x_to=x, core_to=core, y_to=y, zlo_to=zlo):
        return (zhi * 8 + x_to * 2 + core_to, y_to * 4 + zlo_to)

    def copy(number, src, dst, to):
        return pltpu.make_async_remote_copy(
            src_ref=src, dst_ref=dst, send_sem=send_sem.at[number], recv_sem=recv_sem.at[number],
            device_id=to, device_id_type=MESH,
        )

    barrier = pltpu.get_barrier_semaphore()
    partners = [at(core_to=core ^ 1)]
    for d in (1, 2, 3):
        partners += [at(zlo_to=zlo ^ d), at(x_to=x ^ d), at(y_to=y ^ d)]
    for partner in partners:
        pl.semaphore_signal(barrier, inc=1, device_id=partner, device_id_type=MESH)

    convs[zlo] = conv_ref[...]
    biases[zlo, 0:1, :] = cbias_ref[...]
    biases[zlo, 1:2, :] = hbias_ref[...]
    biases[zlo, 2:3, :] = gbias_ref[...]
    weights[zlo, 0:2048, 0:128] = hid_ref[...]
    weights[zlo, 0:2048, 128:256] = gate_ref[...]
    for cb in range(4):
        weights[zlo, 2048 + cb * 128 : 2176 + cb * 128, :] = proj_ref[:, cb * 256 : cb * 256 + 256]

    pl.semaphore_wait(barrier, len(partners))

    sends = []

    def start(number, src, dst, to):
        c = copy(number, src, dst, to)
        c.start()
        sends.append(c)

    mine = pl.ds(pl.multiple_of((core * 4 + x) * CHUNK, CHUNK), CHUNK)
    core_rows = pl.ds(pl.multiple_of(core * 4 * CHUNK, CHUNK), 4 * CHUNK)
    other_rows = pl.ds(pl.multiple_of((core ^ 1) * 4 * CHUNK, CHUNK), 4 * CHUNK)
    for d in (1, 2, 3):
        to = at(zlo_to=zlo ^ d)
        start(d - 1, convs.at[zlo], convs.at[zlo], to)
        start(2 + d, biases.at[zlo], biases.at[zlo], to)
    for d in (1, 2, 3):
        start(5 + d, weights.at[zlo, mine], weights.at[zlo, mine], at(zlo_to=zlo ^ d))

    row = lax.broadcasted_iota(jnp.int32, (BLOCK, GROUP * BLOCK), 0)
    column = lax.broadcasted_iota(jnp.int32, (BLOCK, GROUP * BLOCK), 1)
    source = row + (row // OWN) * (BLOCK - OWN) + zlo * OWN
    chosen = (source == column).astype(F32).astype(BF16)
    spelled = lax.dot_general(
        chosen, ids_ref[...].astype(F32).astype(BF16), (((1,), (1,)), ((), ())),
        preferred_element_type=F32,
    ).astype(jnp.int32)
    letter = lax.broadcasted_iota(jnp.int32, (BLOCK, 256), 1)
    place_row = lax.broadcasted_iota(jnp.int32, (CHAR_DIM, 128), 0)
    place_col = lax.broadcasted_iota(jnp.int32, (CHAR_DIM, 128), 1)
    for j in range(8):
        place = (place_col == place_row + CHAR_DIM * j).astype(F32).astype(BF16)
        tables[j] = dot(table_ref[...], place).astype(BF16)
    for i in range(3):
        total = jnp.zeros((BLOCK, 128), F32)
        for j in range(8):
            p = 8 * i + j
            hot = (spelled[:, p : p + 1] == letter).astype(F32).astype(BF16)
            total += dot(hot, tables[j])
        chars[:, 128 * i : 128 * i + 128] = total.astype(BF16)
    chars[:, 384:512] = jnp.zeros((BLOCK, 128), BF16)

    for d in (1, 2, 3):
        copy(d - 1, convs.at[zlo ^ d], convs.at[zlo ^ d], at(zlo_to=zlo ^ d)).wait_recv()
        copy(2 + d, biases.at[zlo ^ d], biases.at[zlo ^ d], at(zlo_to=zlo ^ d)).wait_recv()
    tap = lax.broadcasted_iota(jnp.int32, (KMAX * CHAR_DIM, WIDE), 0) // CHAR_DIM
    number = y * WIDE + lax.broadcasted_iota(jnp.int32, (KMAX * CHAR_DIM, WIDE), 1)
    keep = tap < 1 + number * KMAX // FILTERS
    filters = jnp.concatenate([convs[q] for q in range(GROUP)], axis=1).astype(F32)
    filters = jnp.where(keep, filters, 0.0).astype(BF16)
    for j in range(8):
        shifted[j] = jnp.zeros((256, WIDE), BF16)
        shifted[j, CHAR_DIM * j : CHAR_DIM * (j + KMAX), :] = filters
    best[...] = jnp.full((BLOCK, WIDE), -3e38, F32)

    def conv_step(j, carry):
        taps = shifted[j]
        top = dot(chars[:, 0:256], taps)
        top = jnp.maximum(top, dot(chars[:, 128:384], taps))
        top = jnp.maximum(top, dot(chars[:, 256:512], taps))
        best[...] = jnp.maximum(best[...], top)
        return carry

    lax.fori_loop(0, 8, conv_step, 0)
    bias = jnp.concatenate([biases[q, 0:1, :] for q in range(GROUP)], axis=1)
    feats[y] = jnp.tanh(best[...] + bias).astype(BF16)
    for d in (1, 2, 3):
        start(8 + d, feats.at[y], feats.at[y], at(y_to=y ^ d))

    for d in (1, 2, 3):
        q = zlo ^ d
        copy(5 + d, weights.at[q, mine], weights.at[q, mine], at(zlo_to=q)).wait_recv()
        for k in (1, 2, 3):
            start(12 + (d - 1) * 3 + k - 1, weights.at[q, mine], weights.at[q, mine], at(x_to=x ^ k))
    for d in (1, 2, 3):
        q = zlo ^ d
        for k in (1, 2, 3):
            theirs = pl.ds(pl.multiple_of((core * 4 + (x ^ k)) * CHUNK, CHUNK), CHUNK)
            copy(
                12 + (d - 1) * 3 + k - 1, weights.at[q, theirs], weights.at[q, theirs], at(x_to=x ^ k)
            ).wait_recv()
        start(20 + d, weights.at[q, core_rows], weights.at[q, core_rows], at(core_to=core ^ 1))
    for d in (1, 2, 3):
        q = zlo ^ d
        copy(20 + d, weights.at[q, other_rows], weights.at[q, other_rows], at(core_to=core ^ 1)).wait_recv()
    for d in (1, 2, 3):
        copy(8 + d, feats.at[y ^ d], feats.at[y ^ d], at(y_to=y ^ d)).wait_recv()

    for q in range(GROUP):
        mixed = dot(feats[0], weights[q, 0:512, :])
        for g in range(1, GROUP):
            mixed += dot(feats[g], weights[q, 512 * g : 512 * g + 512, :])
        hid_in = mixed[:, :128] + biases[q, 1:2, :]
        gate_in = mixed[:, 128:] + biases[q, 2:3, :]
        opened = jax.nn.sigmoid(gate_in)
        carried = feats[y, :, 128 * q : 128 * q + 128].astype(F32)
        highway[:, 128 * q : 128 * q + 128] = (
            opened * jnp.maximum(hid_in, 0.0) + (1.0 - opened) * carried
        ).astype(BF16)

    for cb in range(4):
        matrix = jnp.concatenate(
            [weights[q, 2048 + cb * 128 : 2176 + cb * 128, :] for q in range(GROUP)], axis=0
        )
        product = dot(highway[...], matrix)
        for g in range(GROUP):
            parts[g, :, cb * 256 : cb * 256 + 256] = product[g * OWN : g * OWN + OWN, :].astype(BF16)
    for d in (1, 2, 3):
        start(23 + d, parts.at[y ^ d], arrived.at[d - 1], at(y_to=y ^ d))
    total = parts[y].astype(F32)
    for d in (1, 2, 3):
        copy(23 + d, parts.at[y], arrived.at[d - 1], at(y_to=y ^ d)).wait_recv()
        total += arrived[d - 1].astype(F32)
    out_ref[...] = total.astype(BF16)
    for c in sends:
        c.wait_send()


def build_embeddings(char_ids, char_table, conv_weight, conv_bias, hid, gate, hid_bias, gate_bias, proj):
    vmem = pl.BlockSpec(memory_space=pltpu.VMEM)
    copies = 27
    return pl.pallas_call(
        embed_kernel,
        out_shape=jax.ShapeDtypeStruct((OWN, 1024), BF16),
        in_specs=[vmem] * 9,
        out_specs=vmem,
        scratch_shapes=[
            pltpu.VMEM((GROUP, PACK, 256), BF16),
            pltpu.VMEM((GROUP, KMAX * CHAR_DIM, SLICE), BF16),
            pltpu.VMEM((GROUP, 8, SLICE), F32),
            pltpu.VMEM((8, 256, 128), BF16),
            pltpu.VMEM((BLOCK, 512), BF16),
            pltpu.VMEM((8, 256, WIDE), BF16),
            pltpu.VMEM((BLOCK, WIDE), F32),
            pltpu.VMEM((GROUP, BLOCK, WIDE), BF16),
            pltpu.VMEM((BLOCK, WIDE), BF16),
            pltpu.VMEM((GROUP, OWN, 1024), BF16),
            pltpu.VMEM((GROUP - 1, OWN, 1024), BF16),
            pltpu.SemaphoreType.DMA((copies,)),
            pltpu.SemaphoreType.DMA((copies,)),
        ],
        compiler_params=pltpu.CompilerParams(
            collective_id=0, has_side_effects=True, vmem_limit_bytes=56 << 20
        ),
        name="embed",
    )(
        char_ids, char_table, conv_weight, conv_bias.reshape(1, SLICE), hid, gate,
        hid_bias.reshape(1, SLICE), gate_bias.reshape(1, SLICE), proj,
    )


def score_rows(work, work_targets, bound, embeddings, word_at, row_words, span_rows):
    owner = work_targets % row_words // span_rows
    local_col = work_targets // row_words * span_rows + work_targets % span_rows
    wanted = jnp.where(owner == word_at, local_col, -1)
    row_total_count = work.shape[0]
    block_count = (bound + ROW_BLOCK - 1) // ROW_BLOCK
    initial = (
        jnp.full((row_total_count,), lowest_score, jnp.float32),
        jnp.zeros((row_total_count,), jnp.float32),
        jnp.zeros((row_total_count,), jnp.float32),
    )
    portion = lax.all_gather(embeddings, "tok", axis=0, tiled=True)
    columns = jnp.arange(portion.shape[0], dtype=jnp.int32)

    def one_block(block_id, state):
        row_best, row_total, row_pick = state
        first_row = block_id * ROW_BLOCK
        queries = lax.dynamic_slice_in_dim(work, first_row, ROW_BLOCK, 0)
        scores = lax.dot_general(
            queries, portion, (((1,), (1,)), ((), ())), preferred_element_type=jnp.float32
        )
        old_best = lax.dynamic_slice_in_dim(row_best, first_row, ROW_BLOCK)
        old_total = lax.dynamic_slice_in_dim(row_total, first_row, ROW_BLOCK)
        old_pick = lax.dynamic_slice_in_dim(row_pick, first_row, ROW_BLOCK)
        new_best = jnp.maximum(old_best, jnp.max(scores, axis=1))
        new_total = old_total * jnp.exp(old_best - new_best) + jnp.sum(
            jnp.exp(scores - new_best[:, None]), axis=1
        )
        hits = lax.dynamic_slice_in_dim(wanted, first_row, ROW_BLOCK)[:, None] == columns[None, :]
        new_pick = old_pick + jnp.sum(jnp.where(hits, scores, 0.0), axis=1)
        return (
            lax.dynamic_update_slice_in_dim(row_best, new_best, first_row, 0),
            lax.dynamic_update_slice_in_dim(row_total, new_total, first_row, 0),
            lax.dynamic_update_slice_in_dim(row_pick, new_pick, first_row, 0),
        )

    row_best, row_total, row_pick = lax.fori_loop(0, block_count, one_block, initial)
    top_score = lax.pmax(row_best, "word")
    summed, picked = lax.psum((row_total * jnp.exp(row_best - top_score), row_pick), "word")
    labelled = jnp.arange(row_total_count, dtype=jnp.int32) < bound
    safe_total = jnp.where(labelled, summed, 1.0)
    return jnp.where(labelled, picked - top_score - jnp.log(safe_total), 0.0)


def on_device(
    char_ids,
    char_table,
    conv_weight,
    conv_bias,
    highway_hid,
    highway_gate,
    hid_bias,
    gate_bias,
    proj_weight,
    hidden,
    targets,
    counts,
):
    word_at = lax.axis_index("word")
    tok_at = lax.axis_index("tok")
    embeddings = build_embeddings(
        char_ids, char_table, conv_weight, conv_bias, highway_hid, highway_gate, hid_bias, gate_bias,
        proj_weight,
    )
    own_count = lax.dynamic_index_in_dim(counts, tok_at, keepdims=False)
    own_targets = lax.dynamic_slice_in_dim(targets, tok_at * TOK_DEV, TOK_DEV)
    logprob = score_rows(hidden, own_targets, own_count, embeddings, word_at, GROUP * BLOCK, OWN)
    return (embeddings, logprob)


def solution(mesh):
    return jax.shard_map(
        on_device,
        mesh=mesh,
        in_specs=(
            P(None, "tok"),
            P(),
            P(None, "word"),
            P("word"),
            P(None, "word"),
            P(None, "word"),
            P("word"),
            P("word"),
            P("word", None),
            P("tok", None),
            P(),
            P(),
        ),
        out_specs=(P(("tok", "word"), None), P("tok")),
        check_vma=False,
    )
```

```python
import functools

import jax
import jax.numpy as jnp
from jax import lax
from jax.experimental import pallas as pl
from jax.experimental.pallas import tpu as pltpu
from jax.sharding import PartitionSpec as P

CHAR_DIM = 16
KMAX = 7
CHAR_LEN = 24
FILTERS = 2048
TOK_DEV = 256
MESH = pl.DeviceIdType.MESH
BF16 = jnp.bfloat16
F32 = jnp.float32

GROUP = 4
OWN = 104
BLOCK = GROUP * OWN
SLICE = 128
WIDE = GROUP * SLICE
PACK = 2560
CHUNK = PACK // 8


def dot(a, b, contract=None, precision=None):
    if contract is None:
        return jnp.dot(a, b, preferred_element_type=F32, precision=precision)
    return lax.dot_general(a, b, (contract, ((), ())), preferred_element_type=F32)


def iota(shape, axis):
    return lax.broadcasted_iota(jnp.int32, shape, axis)


def one_hot(condition):
    return condition.astype(F32).astype(BF16)


COPIES = {
    "conv": 3, "bias": 3, "weight_z": 3, "weight_x": 9, "weight_core": 3, "feats": 3, "parts": 3,
    "row_z": 3, "row_zlo": 3, "row_y": 3, "emb_x": 3, "emb_core": 4, "stat_z": 3, "stat_zlo": 3, "stat_y": 3,
}
FIRST, TOTAL = {}, 0
for name, amount in COPIES.items():
    FIRST[name] = TOTAL
    TOTAL += amount


def merge_stats(pieces):
    top = pieces[0][0:1]
    for piece in pieces[1:]:
        top = jnp.maximum(top, piece[0:1])
    total = sum(piece[1:2] * jnp.exp(piece[0:1] - top) for piece in pieces)
    pick = sum(piece[2:3] for piece in pieces)
    return top, total, pick


def whole_kernel(
    counts_ref, ids_ref, table_ref, conv_ref, cbias_ref, hid_ref, gate_ref, hbias_ref, gbias_ref,
    proj_ref, hidden_ref, targets_ref,
    out_ref, logprob_ref,
    weights, convs, biases, tables, chars, shifted, best, feats, highway, parts, arrived,
    pieces, rows, words, scores, stat, zstat, lstat, ystat,
    send_sem, recv_sem,
):
    tok, word = lax.axis_index("tok"), lax.axis_index("word")
    zhi, x, core = tok // 8, (tok // 2) % 4, tok % 2
    y, zlo = word // 4, word % 4

    def at(zhi_to=zhi, x_to=x, core_to=core, y_to=y, zlo_to=zlo):
        return (zhi_to * 8 + x_to * 2 + core_to, y_to * 4 + zlo_to)

    sends = []

    def copy(name, index, src, dst, to):
        number = FIRST[name] + index
        return pltpu.make_async_remote_copy(
            src_ref=src, dst_ref=dst, send_sem=send_sem.at[number], recv_sem=recv_sem.at[number],
            device_id=to, device_id_type=MESH,
        )

    def start(name, index, src, dst, to):
        c = copy(name, index, src, dst, to)
        c.start()
        sends.append(c)

    def arrive(name, index, ref, to):
        copy(name, index, ref, ref, to).wait_recv()

    barrier = pltpu.get_barrier_semaphore()
    partners = [at(core_to=core ^ 1)]
    for d in (1, 2, 3):
        partners += [at(zlo_to=zlo ^ d), at(x_to=x ^ d), at(y_to=y ^ d), at(zhi_to=zhi ^ d)]
    for partner in partners:
        pl.semaphore_signal(barrier, inc=1, device_id=partner, device_id_type=MESH)

    convs[zlo] = conv_ref[...]
    biases[zlo, 0:1, :] = cbias_ref[...]
    biases[zlo, 1:2, :] = hbias_ref[...]
    biases[zlo, 2:3, :] = gbias_ref[...]
    weights[zlo, 0:2048, 0:128] = hid_ref[...]
    weights[zlo, 0:2048, 128:256] = gate_ref[...]
    for cb in range(4):
        weights[zlo, 2048 + cb * 128 : 2176 + cb * 128, :] = proj_ref[:, cb * 256 : cb * 256 + 256]
    place = word * 16 + iota((16, TOK_DEV), 0)
    place = jnp.where(zhi >= 2, TOK_DEV - 1 - place, place)
    pieces[zhi] = dot(one_hot(place == iota((16, TOK_DEV), 1)), hidden_ref[...]).astype(BF16)

    row = iota((BLOCK, 1), 0)
    block = (row >= OWN).astype(jnp.int32) + (row >= 2 * OWN).astype(jnp.int32) + (row >= 3 * OWN).astype(jnp.int32)
    source = row + block * (BLOCK - OWN) + zlo * OWN
    chosen = one_hot(source == iota((BLOCK, GROUP * BLOCK), 1))
    spelled = dot(chosen, ids_ref[...].astype(F32).astype(BF16), ((1,), (1,))).astype(jnp.int32)
    letter = iota((BLOCK, 256), 1)
    for j in range(8):
        shift = one_hot(iota((CHAR_DIM, 128), 1) == iota((CHAR_DIM, 128), 0) + CHAR_DIM * j)
        tables[j] = dot(table_ref[...], shift).astype(BF16)
    for i in range(3):
        total = jnp.zeros((BLOCK, 128), F32)
        for j in range(8):
            p = 8 * i + j
            total += dot(one_hot(spelled[:, p : p + 1] == letter), tables[j])
        chars[:, 128 * i : 128 * i + 128] = total.astype(BF16)
    chars[:, 384:512] = jnp.zeros((BLOCK, 128), BF16)

    pl.semaphore_wait(barrier, len(partners))

    mine = pl.ds(pl.multiple_of((core * 4 + x) * CHUNK, CHUNK), CHUNK)
    core_rows = pl.ds(pl.multiple_of(core * 4 * CHUNK, CHUNK), 4 * CHUNK)
    other_rows = pl.ds(pl.multiple_of((core ^ 1) * 4 * CHUNK, CHUNK), 4 * CHUNK)
    for d in (1, 2, 3):
        to = at(zlo_to=zlo ^ d)
        start("conv", d - 1, convs.at[zlo], convs.at[zlo], to)
        start("bias", d - 1, biases.at[zlo], biases.at[zlo], to)
    for d in (1, 2, 3):
        start("weight_z", d - 1, weights.at[zlo, mine], weights.at[zlo, mine], at(zlo_to=zlo ^ d))
    for d in (1, 2, 3):
        start("row_z", d - 1, pieces.at[zhi], pieces.at[zhi], at(zhi_to=zhi ^ d))

    for d in (1, 2, 3):
        arrive("conv", d - 1, convs.at[zlo ^ d], at(zlo_to=zlo ^ d))
        arrive("bias", d - 1, biases.at[zlo ^ d], at(zlo_to=zlo ^ d))
    tap = iota((KMAX * CHAR_DIM, WIDE), 0) >> 4
    number = y * WIDE + iota((KMAX * CHAR_DIM, WIDE), 1)
    keep = tap < 1 + ((number * KMAX) >> 11)
    filters = jnp.concatenate([convs[q] for q in range(GROUP)], axis=1).astype(F32)
    filters = jnp.where(keep, filters, 0.0).astype(BF16)
    for j in range(8):
        shifted[j] = jnp.zeros((256, WIDE), BF16)
        shifted[j, CHAR_DIM * j : CHAR_DIM * (j + KMAX), :] = filters
    best[...] = jnp.full((BLOCK, WIDE), -3e38, F32)

    def conv_step(j, carry):
        taps = shifted[j]
        top = dot(chars[:, 0:256], taps)
        top = jnp.maximum(top, dot(chars[:, 128:384], taps))
        top = jnp.maximum(top, dot(chars[:, 256:512], taps))
        best[...] = jnp.maximum(best[...], top)
        return carry

    lax.fori_loop(0, 8, conv_step, 0)
    bias = jnp.concatenate([biases[q, 0:1, :] for q in range(GROUP)], axis=1)
    feats[y] = jnp.tanh(best[...] + bias).astype(BF16)
    for d in (1, 2, 3):
        start("feats", d - 1, feats.at[y], feats.at[y], at(y_to=y ^ d))

    for d in (1, 2, 3):
        q = zlo ^ d
        arrive("weight_z", d - 1, weights.at[q, mine], at(zlo_to=q))
        for k in (1, 2, 3):
            start("weight_x", (d - 1) * 3 + k - 1, weights.at[q, mine], weights.at[q, mine], at(x_to=x ^ k))

    own_rows = pl.ds(pl.multiple_of(word * 16, 16), 16)
    y_rows = pl.ds(pl.multiple_of(y * 64, 64), 64)
    for d in (1, 2, 3):
        arrive("row_z", d - 1, pieces.at[zhi ^ d], at(zhi_to=zhi ^ d))
    position = word * 16 + iota((16, 1024), 0)
    for a in range(2):
        lower = position < counts_ref[a * 8 + x * 2 + core]
        rows[a, own_rows, :] = jnp.where(
            lower, pieces[a].astype(F32), pieces[a + 2].astype(F32)
        ).astype(BF16)
    for d in (1, 2, 3):
        start("row_zlo", d - 1, rows.at[:, own_rows], rows.at[:, own_rows], at(zlo_to=zlo ^ d))

    flip = one_hot(iota((TOK_DEV, TOK_DEV), 0) + iota((TOK_DEV, TOK_DEV), 1) == TOK_DEV - 1)
    lane = iota((1, TOK_DEV), 1)
    wanted = []
    for a in range(2):
        shard = a * 8 + x * 2 + core
        upper = targets_ref[pl.ds(shard + 16, 1), :]
        high, low = upper >> 8, upper & 255
        high = dot(high.astype(F32).astype(BF16), flip).astype(jnp.int32)
        low = dot(low.astype(F32).astype(BF16), flip).astype(jnp.int32)
        target = jnp.where(lane < counts_ref[shard], targets_ref[pl.ds(shard, 1), :], high * 256 + low)
        owner = target // (GROUP * BLOCK)
        rest = target - owner * (GROUP * BLOCK)
        slot = rest // OWN
        here = ((owner >> 3) == zhi) & (slot == word)
        local = (owner & 1) * BLOCK + ((owner >> 1) & 3) * OWN + rest - slot * OWN
        wanted.append(jnp.where(here, local, -1))
    wanted = jnp.concatenate(wanted, axis=1)

    for d in (1, 2, 3):
        q = zlo ^ d
        for k in (1, 2, 3):
            theirs = pl.ds(pl.multiple_of((core * 4 + (x ^ k)) * CHUNK, CHUNK), CHUNK)
            arrive("weight_x", (d - 1) * 3 + k - 1, weights.at[q, theirs], at(x_to=x ^ k))
        start("weight_core", d - 1, weights.at[q, core_rows], weights.at[q, core_rows], at(core_to=core ^ 1))
    for d in (1, 2, 3):
        arrive("weight_core", d - 1, weights.at[zlo ^ d, other_rows], at(core_to=core ^ 1))
    for d in (1, 2, 3):
        arrive("feats", d - 1, feats.at[y ^ d], at(y_to=y ^ d))

    for q in range(GROUP):
        mixed = dot(feats[0], weights[q, 0:512, :])
        for g in range(1, GROUP):
            mixed += dot(feats[g], weights[q, 512 * g : 512 * g + 512, :])
        hid_in = mixed[:, :128] + biases[q, 1:2, :]
        gate_in = mixed[:, 128:] + biases[q, 2:3, :]
        opened = jax.nn.sigmoid(gate_in)
        carried = feats[y, :, 128 * q : 128 * q + 128].astype(F32)
        highway[:, 128 * q : 128 * q + 128] = (
            opened * jnp.maximum(hid_in, 0.0) + (1.0 - opened) * carried
        ).astype(BF16)

    for cb in range(4):
        matrix = jnp.concatenate(
            [weights[q, 2048 + cb * 128 : 2176 + cb * 128, :] for q in range(GROUP)], axis=0
        )
        product = dot(highway[...], matrix)
        for g in range(GROUP):
            parts[g, :, cb * 256 : cb * 256 + 256] = product[g * OWN : g * OWN + OWN, :].astype(BF16)
    for d in (1, 2, 3):
        start("parts", d - 1, parts.at[y ^ d], arrived.at[d - 1], at(y_to=y ^ d))
    for d in (1, 2, 3):
        theirs = pl.ds(pl.multiple_of(y * 64 + (zlo ^ d) * 16, 16), 16)
        arrive("row_zlo", d - 1, rows.at[:, theirs], at(zlo_to=zlo ^ d))
    for d in (1, 2, 3):
        start("row_y", d - 1, rows.at[:, y_rows], rows.at[:, y_rows], at(y_to=y ^ d))
    total = parts[y].astype(F32)
    for d in (1, 2, 3):
        arrive("parts", d - 1, arrived.at[d - 1], at(y_to=y ^ d))
        total += arrived[d - 1].astype(F32)
    own_words = total.astype(BF16)
    out_ref[...] = own_words
    words[core, x] = own_words
    for k in (1, 2, 3):
        start("emb_x", k - 1, words.at[core, x], words.at[core, x], at(x_to=x ^ k))
    start("emb_core", 0, words.at[core, x], words.at[core, x], at(core_to=core ^ 1))
    for d in (1, 2, 3):
        theirs = pl.ds(pl.multiple_of((y ^ d) * 64, 64), 64)
        arrive("row_y", d - 1, rows.at[:, theirs], at(y_to=y ^ d))
    for k in (1, 2, 3):
        arrive("emb_x", k - 1, words.at[core, x ^ k], at(x_to=x ^ k))
        start("emb_core", k, words.at[core, x ^ k], words.at[core, x ^ k], at(core_to=core ^ 1))

    queries = rows[...].reshape(2 * TOK_DEV, 1024)

    def score(side):
        values = dot(words[side].reshape(BLOCK, 1024), queries, ((1,), (1,)))
        scores[...] = values
        values = scores[...]
        top = jnp.max(values, axis=0, keepdims=True)
        total = jnp.sum(jnp.exp(values - top), axis=0, keepdims=True)
        hits = iota((BLOCK, 2 * TOK_DEV), 0) == wanted - side * BLOCK
        pick = jnp.sum(jnp.where(hits, values, 0.0), axis=0, keepdims=True)
        return jnp.concatenate([top, total, pick], axis=0)

    near = score(core)
    arrive("emb_core", 0, words.at[core ^ 1, x], at(core_to=core ^ 1))
    for k in (1, 2, 3):
        arrive("emb_core", k, words.at[core ^ 1, x ^ k], at(core_to=core ^ 1))
    far = score(core ^ 1)

    def keep_stats(ref, at_rows, values):
        top, total, pick = values
        ref[at_rows + (slice(0, 1), slice(None))] = top
        ref[at_rows + (slice(1, 2), slice(None))] = total
        ref[at_rows + (slice(2, 3), slice(None))] = pick

    stat[...] = jnp.zeros((8, 2 * TOK_DEV), F32)
    keep_stats(stat, (), merge_stats([near, far]))

    def half(z):
        return pl.ds(pl.multiple_of((z % 2) * TOK_DEV, TOK_DEV), TOK_DEV)

    for d in (1, 2, 3):
        start("stat_z", d - 1, stat.at[:, half(zhi ^ d)], zstat.at[zhi], at(zhi_to=zhi ^ d))
    zstat[zhi] = stat[:, half(zhi)]
    for d in (1, 2, 3):
        arrive("stat_z", d - 1, zstat.at[zhi ^ d], at(zhi_to=zhi ^ d))
    lstat[zlo] = jnp.zeros((8, TOK_DEV), F32)
    keep_stats(lstat, (zlo,), merge_stats([zstat[n] for n in range(4)]))
    for d in (1, 2, 3):
        start("stat_zlo", d - 1, lstat.at[zlo], lstat.at[zlo], at(zlo_to=zlo ^ d))
    for d in (1, 2, 3):
        arrive("stat_zlo", d - 1, lstat.at[zlo ^ d], at(zlo_to=zlo ^ d))
    ystat[y] = jnp.zeros((8, TOK_DEV), F32)
    keep_stats(ystat, (y,), merge_stats([lstat[n] for n in range(4)]))
    for d in (1, 2, 3):
        start("stat_y", d - 1, ystat.at[y], ystat.at[y], at(y_to=y ^ d))
    for d in (1, 2, 3):
        arrive("stat_y", d - 1, ystat.at[y ^ d], at(y_to=y ^ d))
    top, total, pick = merge_stats([ystat[n] for n in range(4)])
    result = pick - (top + jnp.log(total))
    first = result.astype(BF16)
    left = result - first.astype(F32)
    second = left.astype(BF16)
    third = (left - second.astype(F32)).astype(BF16)
    turned = dot(first, flip) + dot(second, flip) + dot(third, flip)
    result = jnp.where(zhi >= 2, turned, result)
    logprob_ref[...] = jnp.where(lane < counts_ref[tok], result, 0.0)
    for c in sends:
        c.wait_send()


def on_device(
    char_ids,
    char_table,
    conv_weight,
    conv_bias,
    highway_hid,
    highway_gate,
    hid_bias,
    gate_bias,
    proj_weight,
    hidden,
    targets,
    counts,
):
    vmem = pl.BlockSpec(memory_space=pltpu.VMEM)
    embeddings, logprob = pl.pallas_call(
        whole_kernel,
        out_shape=(
            jax.ShapeDtypeStruct((OWN, 1024), BF16),
            jax.ShapeDtypeStruct((1, TOK_DEV), F32),
        ),
        in_specs=[pl.BlockSpec(memory_space=pltpu.SMEM)] + [vmem] * 11,
        out_specs=(vmem, vmem),
        scratch_shapes=[
            pltpu.VMEM((GROUP, PACK, 256), BF16),
            pltpu.VMEM((GROUP, KMAX * CHAR_DIM, SLICE), BF16),
            pltpu.VMEM((GROUP, 8, SLICE), F32),
            pltpu.VMEM((8, 256, 128), BF16),
            pltpu.VMEM((BLOCK, 512), BF16),
            pltpu.VMEM((8, 256, WIDE), BF16),
            pltpu.VMEM((BLOCK, WIDE), F32),
            pltpu.VMEM((GROUP, BLOCK, WIDE), BF16),
            pltpu.VMEM((BLOCK, WIDE), BF16),
            pltpu.VMEM((GROUP, OWN, 1024), BF16),
            pltpu.VMEM((GROUP - 1, OWN, 1024), BF16),
            pltpu.VMEM((4, 16, 1024), BF16),
            pltpu.VMEM((2, TOK_DEV, 1024), BF16),
            pltpu.VMEM((2, GROUP, OWN, 1024), BF16),
            pltpu.VMEM((BLOCK, 2 * TOK_DEV), F32),
            pltpu.VMEM((8, 2 * TOK_DEV), F32),
            pltpu.VMEM((4, 8, TOK_DEV), F32),
            pltpu.VMEM((4, 8, TOK_DEV), F32),
            pltpu.VMEM((4, 8, TOK_DEV), F32),
            pltpu.SemaphoreType.DMA((TOTAL,)),
            pltpu.SemaphoreType.DMA((TOTAL,)),
        ],
        compiler_params=pltpu.CompilerParams(
            collective_id=0, has_side_effects=True, vmem_limit_bytes=56 << 20
        ),
        name="whole",
    )(
        counts, char_ids, char_table, conv_weight, conv_bias.reshape(1, SLICE), highway_hid, highway_gate,
        hid_bias.reshape(1, SLICE), gate_bias.reshape(1, SLICE), proj_weight, hidden,
        targets.reshape(32, TOK_DEV),
    )
    return embeddings, logprob.reshape(TOK_DEV)


def solution(mesh):
    return jax.shard_map(
        on_device,
        mesh=mesh,
        in_specs=(
            P(None, "tok"),
            P(),
            P(None, "word"),
            P("word"),
            P(None, "word"),
            P(None, "word"),
            P("word"),
            P("word"),
            P("word", None),
            P("tok", None),
            P(),
            P(),
        ),
        out_specs=(P(("tok", "word"), None), P("tok")),
        check_vma=False,
    )
```

```python
import functools

import jax
import jax.numpy as jnp
from jax import lax
from jax.experimental import pallas as pl
from jax.experimental.pallas import tpu as pltpu
from jax.sharding import PartitionSpec as P

CHAR_DIM = 16
KMAX = 7
CHAR_LEN = 24
FILTERS = 2048
TOK_DEV = 256
MESH = pl.DeviceIdType.MESH
BF16 = jnp.bfloat16
F32 = jnp.float32

GROUP = 4
OWN = 104
BLOCK = GROUP * OWN
SLICE = 128
WIDE = GROUP * SLICE
PACK = 2560
PIECE = PACK // 16
HALF = BLOCK // 2
CHUNKS = 2
WIDTH = 1024 // CHUNKS


def dot(a, b, contract=None, precision=None):
    if contract is None:
        return jnp.dot(a, b, preferred_element_type=F32, precision=precision)
    return lax.dot_general(a, b, (contract, ((), ())), preferred_element_type=F32)


def iota(shape, axis):
    return lax.broadcasted_iota(jnp.int32, shape, axis)


def one_hot(condition):
    return condition.astype(F32).astype(BF16)


COPIES = {
    "conv": 3, "bias": 3, "weight_z": 6, "weight_x": 12, "weight_far": 6, "weight_core": 6,
    "feats": 4, "feats_far": 2, "parts": 3 * CHUNKS, "row_z": 3, "row_zlo": 3, "row_y": 2, "row_far": 2,
    "emb_x": 2 * CHUNKS, "emb_far": CHUNKS, "emb_core": CHUNKS, "stat_z": 15, "stat_y": 3,
}
FIRST, TOTAL = {}, 0
for name, amount in COPIES.items():
    FIRST[name] = TOTAL
    TOTAL += amount


def merge_stats(pieces):
    half = pieces[0].shape[0] // 2
    top = pieces[0][:half]
    for piece in pieces[1:]:
        top = jnp.maximum(top, piece[:half])
    total = sum(jnp.exp(piece[:half] - top) for piece in pieces)
    pick = sum(piece[half:] for piece in pieces)
    return jnp.concatenate([top + jnp.log(total), pick], axis=0)


def whole_kernel(
    counts_ref, ids_ref, table_ref, conv_ref, cbias_ref, hid_ref, gate_ref, hbias_ref, gbias_ref,
    proj_ref, hidden_ref, targets_ref,
    out_ref, logprob_ref,
    weights, convs, biases, tables, chars, shifted, best, feats, highway, parts, arrived,
    pieces, rows, words, scores, stat, zstat, ystat,
    send_sem, recv_sem,
):
    tok, word = lax.axis_index("tok"), lax.axis_index("word")
    zhi, x, core = tok // 8, (tok // 2) % 4, tok % 2
    y, zlo = word // 4, word % 4

    def at(zhi_to=zhi, x_to=x, core_to=core, y_to=y, zlo_to=zlo):
        return (zhi_to * 8 + x_to * 2 + core_to, y_to * 4 + zlo_to)

    sends = []

    def copy(name, index, src, dst, to):
        number = FIRST[name] + index
        return pltpu.make_async_remote_copy(
            src_ref=src, dst_ref=dst, send_sem=send_sem.at[number], recv_sem=recv_sem.at[number],
            device_id=to, device_id_type=MESH,
        )

    def start(name, index, src, dst, to):
        c = copy(name, index, src, dst, to)
        c.start()
        sends.append(c)

    def arrive(name, index, ref, to):
        copy(name, index, ref, ref, to).wait_recv()

    barrier = pltpu.get_barrier_semaphore()
    partners = [at(core_to=core ^ 1)]
    for d in (1, 2, 3):
        partners += [at(x_to=x ^ d), at(y_to=y ^ d)]
    partners += [at(zhi_to=zhi ^ (d >> 2), zlo_to=zlo ^ (d & 3)) for d in range(1, 16)]
    for partner in partners:
        pl.semaphore_signal(barrier, inc=1, device_id=partner, device_id_type=MESH)

    convs[zlo] = conv_ref[...]
    biases[zlo, 0:1, :] = cbias_ref[...]
    biases[zlo, 1:2, :] = hbias_ref[...]
    biases[zlo, 2:3, :] = gbias_ref[...]
    weights[zlo, 0:2048, 0:128] = hid_ref[...]
    weights[zlo, 0:2048, 128:256] = gate_ref[...]
    for cb in range(4):
        weights[zlo, 2048 + cb * 128 : 2176 + cb * 128, :] = proj_ref[:, cb * 256 : cb * 256 + 256]
    place = word * 16 + iota((16, TOK_DEV), 0)
    place = jnp.where(zhi >= 2, TOK_DEV - 1 - place, place)
    pieces[zhi] = dot(one_hot(place == iota((16, TOK_DEV), 1)), hidden_ref[...]).astype(BF16)

    row = iota((BLOCK, 1), 0)
    block = (row >= OWN).astype(jnp.int32) + (row >= 2 * OWN).astype(jnp.int32) + (row >= 3 * OWN).astype(jnp.int32)
    source = row + block * (BLOCK - OWN) + zlo * OWN
    chosen = one_hot(source == iota((BLOCK, GROUP * BLOCK), 1))
    spelled = dot(chosen, ids_ref[...].astype(F32).astype(BF16), ((1,), (1,))).astype(jnp.int32)
    letter = iota((BLOCK, 256), 1)
    for j in range(8):
        shift = one_hot(iota((CHAR_DIM, 128), 1) == iota((CHAR_DIM, 128), 0) + CHAR_DIM * j)
        tables[j] = dot(table_ref[...], shift, ((0,), (0,))).astype(BF16)
    for i in range(3):
        total = jnp.zeros((BLOCK, 128), F32)
        for j in range(8):
            p = 8 * i + j
            total += dot(one_hot(spelled[:, p : p + 1] == letter), tables[j])
        chars[:, 128 * i : 128 * i + 128] = total.astype(BF16)
    chars[:, 384:512] = jnp.zeros((BLOCK, 128), BF16)

    pl.semaphore_wait(barrier, len(partners))

    x_next, x_last, x_far = (x + 1) % 4, (x + 3) % 4, (x + 2) % 4
    y_next, y_last, y_far = (y + 1) % 4, (y + 3) % 4, (y + 2) % 4

    def piece(part, x_of):
        return pl.ds(pl.multiple_of(part * (PACK // 2) + core * (4 * PIECE) + x_of * PIECE, PIECE), PIECE)

    def core_pieces(part, core_of):
        return pl.ds(pl.multiple_of(part * (PACK // 2) + core_of * (4 * PIECE), 4 * PIECE), 4 * PIECE)

    def start_weights(part):
        for d in (1, 2, 3):
            ref = weights.at[zlo, piece(part, x)]
            start("weight_z", part * 3 + d - 1, ref, ref, at(zlo_to=zlo ^ d))

    for d in (1, 2, 3):
        to = at(zlo_to=zlo ^ d)
        start("conv", d - 1, convs.at[zlo], convs.at[zlo], to)
        start("bias", d - 1, biases.at[zlo], biases.at[zlo], to)
    start_weights(0)
    start_weights(1)
    for d in (1, 2, 3):
        start("row_z", d - 1, pieces.at[zhi], pieces.at[zhi], at(zhi_to=zhi ^ d))

    for d in (1, 2, 3):
        arrive("conv", d - 1, convs.at[zlo ^ d], at(zlo_to=zlo ^ d))
        arrive("bias", d - 1, biases.at[zlo ^ d], at(zlo_to=zlo ^ d))
    tap = iota((KMAX * CHAR_DIM, WIDE), 0) >> 4
    number = y * WIDE + iota((KMAX * CHAR_DIM, WIDE), 1)
    keep = tap < 1 + ((number * KMAX) >> 11)
    filters = jnp.concatenate([convs[q] for q in range(GROUP)], axis=1).astype(F32)
    filters = jnp.where(keep, filters, 0.0).astype(BF16)
    for j in range(8):
        shifted[j] = jnp.zeros((256, WIDE), BF16)
        shifted[j, CHAR_DIM * j : CHAR_DIM * (j + KMAX), :] = filters
    best[...] = jnp.full((BLOCK, WIDE), -3e38, F32)

    bias = jnp.concatenate([biases[q, 0:1, :] for q in range(GROUP)], axis=1)
    for h in range(2):
        low, high = h * HALF, h * HALF + HALF

        def conv_step(j, carry):
            taps = shifted[j]
            top = dot(chars[low:high, 0:256], taps)
            top = jnp.maximum(top, dot(chars[low:high, 128:384], taps))
            top = jnp.maximum(top, dot(chars[low:high, 256:512], taps))
            best[low:high, :] = jnp.maximum(best[low:high, :], top)
            return carry

        lax.fori_loop(0, 8, conv_step, 0)
        feats[y, low:high, :] = jnp.tanh(best[low:high, :] + bias).astype(BF16)
        ref = feats.at[y, low:high]
        start("feats", h, ref, ref, at(y_to=y_next))
        start("feats", 2 + h, ref, ref, at(y_to=y_last))

    def weights_to_x(part):
        for d in (1, 2, 3):
            ref = weights.at[zlo ^ d, piece(part, x)]
            arrive("weight_z", part * 3 + d - 1, ref, at(zlo_to=zlo ^ d))
            start("weight_x", part * 6 + d - 1, ref, ref, at(x_to=x_next))
            start("weight_x", part * 6 + 2 + d, ref, ref, at(x_to=x_last))

    def weights_far(part):
        neighbour, other, base = ((x_last, x_next, 0), (x_next, x_last, 9))[part]
        for d in (1, 2, 3):
            ref = weights.at[zlo ^ d, piece(part, neighbour)]
            arrive("weight_x", base + d - 1, ref, at(x_to=neighbour))
            start("weight_far", part * 3 + d - 1, ref, ref, at(x_to=other))

    def feats_far(h):
        neighbour, other = ((y_last, y_next), (y_next, y_last))[h]
        ref = feats.at[neighbour, h * HALF : h * HALF + HALF]
        arrive("feats", 3 * h, ref, at(y_to=neighbour))
        start("feats_far", h, ref, ref, at(y_to=other))

    weights_to_x(0)
    feats_far(0)
    weights_to_x(1)
    feats_far(1)
    weights_far(0)
    weights_far(1)

    own_rows = pl.ds(pl.multiple_of(word * 16, 16), 16)

    def y_rows(y_of):
        return pl.ds(pl.multiple_of(y_of * 64, 64), 64)

    for d in (1, 2, 3):
        arrive("row_z", d - 1, pieces.at[zhi ^ d], at(zhi_to=zhi ^ d))
    position = word * 16 + iota((16, 1024), 0)
    for a in range(2):
        lower = position < counts_ref[a * 8 + x * 2 + core]
        rows[a, own_rows, :] = jnp.where(
            lower, pieces[a].astype(F32), pieces[a + 2].astype(F32)
        ).astype(BF16)
    for d in (1, 2, 3):
        start("row_zlo", d - 1, rows.at[:, own_rows], rows.at[:, own_rows], at(zlo_to=zlo ^ d))

    flip = one_hot(iota((TOK_DEV, TOK_DEV), 0) + iota((TOK_DEV, TOK_DEV), 1) == TOK_DEV - 1)
    lane = iota((1, TOK_DEV), 1)

    def shard_targets(shard):
        both = targets_ref[pl.ds(2 * shard, 2), :]
        return jnp.concatenate([both[0:1, :], both[1:2, :]], axis=1)

    wanted = []
    for a in range(2):
        shard = a * 8 + x * 2 + core
        upper = shard_targets(shard + 16)
        high, low = upper >> 8, upper & 255
        high = dot(high.astype(F32).astype(BF16), flip).astype(jnp.int32)
        low = dot(low.astype(F32).astype(BF16), flip).astype(jnp.int32)
        target = jnp.where(lane < counts_ref[shard], shard_targets(shard), high * 256 + low)
        owner = target // (GROUP * BLOCK)
        rest = target - owner * (GROUP * BLOCK)
        slot = rest // OWN
        here = ((owner >> 3) == zhi) & (slot == word)
        local = ((owner & 1) ^ core) * BLOCK + ((owner >> 1) & 3) * OWN + rest - slot * OWN
        wanted.append(jnp.where(here, local, -1))
    wanted = jnp.concatenate(wanted, axis=1)

    for d in (1, 2, 3):
        theirs = pl.ds(pl.multiple_of(y * 64 + (zlo ^ d) * 16, 16), 16)
        arrive("row_zlo", d - 1, rows.at[:, theirs], at(zlo_to=zlo ^ d))
    ref = rows.at[:, y_rows(y)]
    start("row_y", 0, ref, ref, at(y_to=y_next))
    start("row_y", 1, ref, ref, at(y_to=y_last))

    for part, neighbour, base in ((0, x_next, 3), (1, x_last, 6)):
        for d in (1, 2, 3):
            q = zlo ^ d
            arrive("weight_x", base + d - 1, weights.at[q, piece(part, neighbour)], at(x_to=neighbour))
            arrive("weight_far", part * 3 + d - 1, weights.at[q, piece(part, x_far)], at(x_to=neighbour))
            ref = weights.at[q, core_pieces(part, core)]
            start("weight_core", part * 3 + d - 1, ref, ref, at(core_to=core ^ 1))
    arrive("feats", 1, feats.at[y_last, HALF:BLOCK], at(y_to=y_last))
    arrive("feats", 2, feats.at[y_next, 0:HALF], at(y_to=y_next))
    arrive("feats_far", 0, feats.at[y_far, 0:HALF], at(y_to=y_last))
    arrive("feats_far", 1, feats.at[y_far, HALF:BLOCK], at(y_to=y_next))

    for d in range(4):
        q = zlo ^ d
        if d:
            for part in range(2):
                ref = weights.at[q, core_pieces(part, core ^ 1)]
                arrive("weight_core", part * 3 + d - 1, ref, at(core_to=core ^ 1))
        mixed = dot(feats[0], weights[q, 0:512, :])
        for g in range(1, GROUP):
            mixed += dot(feats[g], weights[q, 512 * g : 512 * g + 512, :])
        hid_in = mixed[:, :128] + biases[q, 1:2, :]
        gate_in = mixed[:, 128:] + biases[q, 2:3, :]
        opened = jax.nn.sigmoid(gate_in)
        columns = pl.ds(pl.multiple_of(q * SLICE, SLICE), SLICE)
        carried = feats[y, :, columns].astype(F32)
        highway[:, columns] = (opened * jnp.maximum(hid_in, 0.0) + (1.0 - opened) * carried).astype(BF16)

    for c in range(CHUNKS):
        for cb in range(c * WIDTH // 256, (c + 1) * WIDTH // 256):
            matrix = jnp.concatenate(
                [weights[q, 2048 + cb * 128 : 2176 + cb * 128, :] for q in range(GROUP)], axis=0
            )
            product = dot(highway[...], matrix).astype(BF16)
            column = cb * 256 - c * WIDTH
            for g in range(GROUP):
                parts[c, g, :, column : column + 256] = product[g * OWN : g * OWN + OWN, :]
        for d in (1, 2, 3):
            start("parts", 3 * c + d - 1, parts.at[c, y ^ d], arrived.at[c, d - 1], at(y_to=y ^ d))

    arrive("row_y", 0, rows.at[:, y_rows(y_last)], at(y_to=y_last))
    ref = rows.at[0, y_rows(y_last)]
    start("row_far", 0, ref, ref, at(y_to=y_next))
    arrive("row_y", 1, rows.at[:, y_rows(y_next)], at(y_to=y_next))
    ref = rows.at[1, y_rows(y_next)]
    start("row_far", 1, ref, ref, at(y_to=y_last))

    def sum_chunk(c):
        total = parts[c, y].astype(F32)
        for d in (1, 2, 3):
            arrive("parts", 3 * c + d - 1, arrived.at[c, d - 1], at(y_to=y ^ d))
            total += arrived[c, d - 1].astype(F32)
        own_words = total.astype(BF16)
        out_ref[:, c * WIDTH : c * WIDTH + WIDTH] = own_words
        words[core, c, x] = own_words
        ref = words.at[core, c, x]
        start("emb_x", 2 * c, ref, ref, at(x_to=x_next))
        start("emb_x", 2 * c + 1, ref, ref, at(x_to=x_last))

    def forward_chunk(c):
        arrive("emb_x", 2 * c, words.at[core, c, x_last], at(x_to=x_last))
        if c % 2 == 0:
            ref = words.at[core, c, x_last]
            start("emb_far", c, ref, ref, at(x_to=x_next))
        arrive("emb_x", 2 * c + 1, words.at[core, c, x_next], at(x_to=x_next))
        if c % 2 == 1:
            ref = words.at[core, c, x_next]
            start("emb_far", c, ref, ref, at(x_to=x_last))

    def share_chunk(c):
        arrive("emb_far", c, words.at[core, c, x_far], at(x_to=x_last if c % 2 == 0 else x_next))
        start("emb_core", c, words.at[core, c], words.at[core, c], at(core_to=core ^ 1))

    def score_side(c, side):
        queries = rows[:, :, c * WIDTH : c * WIDTH + WIDTH].reshape(2 * TOK_DEV, WIDTH)
        values = dot(words[core ^ side, c].reshape(BLOCK, WIDTH), queries, ((1,), (1,)))
        scores[side] = values if c == 0 else scores[side] + values

    def score_chunk(c):
        if c == 0:
            arrive("row_far", 0, rows.at[0, y_rows(y_far)], at(y_to=y_last))
            arrive("row_far", 1, rows.at[1, y_rows(y_far)], at(y_to=y_next))
        score_side(c, 0)
        arrive("emb_core", c, words.at[core ^ 1, c], at(core_to=core ^ 1))
        score_side(c, 1)

    for step in range(CHUNKS + 4):
        for lag, action in ((0, sum_chunk), (2, forward_chunk), (3, share_chunk), (4, score_chunk)):
            if 0 <= step - lag < CHUNKS:
                action(step - lag)

    def statistics(side):
        values = scores[side]
        top = jnp.max(values, axis=0, keepdims=True)
        total = jnp.sum(jnp.exp(values - top), axis=0, keepdims=True)
        hits = iota((BLOCK, 2 * TOK_DEV), 0) == wanted - side * BLOCK
        pick = jnp.sum(jnp.where(hits, values, 0.0), axis=0, keepdims=True)
        return jnp.concatenate([top + jnp.log(total), pick], axis=0)

    both = merge_stats([statistics(0), statistics(1)])
    for a in range(2):
        for r in range(2):
            first = a * TOK_DEV + r * 128
            stat[a, r : r + 1, :] = both[0:1, first : first + 128]
            stat[a, r + 2 : r + 3, :] = both[1:2, first : first + 128]
    for d in range(1, 16):
        z_to = zhi ^ (d >> 2)
        start(
            "stat_z", d - 1, stat.at[z_to % 2], zstat.at[zhi * 4 + zlo],
            at(zhi_to=z_to, zlo_to=zlo ^ (d & 3)),
        )
    zstat[zhi * 4 + zlo] = stat[zhi % 2]
    for d in range(1, 16):
        z_of, l_of = zhi ^ (d >> 2), zlo ^ (d & 3)
        arrive("stat_z", d - 1, zstat.at[z_of * 4 + l_of], at(zhi_to=z_of, zlo_to=l_of))
    ystat[y] = merge_stats([zstat[n] for n in range(16)])
    for d in (1, 2, 3):
        start("stat_y", d - 1, ystat.at[y], ystat.at[y], at(y_to=y ^ d))
    for d in (1, 2, 3):
        arrive("stat_y", d - 1, ystat.at[y ^ d], at(y_to=y ^ d))
    both = merge_stats([ystat[n] for n in range(4)])
    result = both[2:4] - both[0:2]
    result = jnp.concatenate([result[0:1], result[1:2]], axis=1)
    first = result.astype(BF16)
    left = result - first.astype(F32)
    second = left.astype(BF16)
    third = (left - second.astype(F32)).astype(BF16)
    turned = dot(first, flip) + dot(second, flip) + dot(third, flip)
    result = jnp.where(zhi >= 2, turned, result)
    result = jnp.where(lane < counts_ref[tok], result, 0.0)
    logprob_ref[0:1, :] = result[:, 0:128]
    logprob_ref[1:2, :] = result[:, 128:256]
    for c in sends:
        c.wait_send()


def on_device(
    char_ids,
    char_table,
    conv_weight,
    conv_bias,
    highway_hid,
    highway_gate,
    hid_bias,
    gate_bias,
    proj_weight,
    hidden,
    targets,
    counts,
):
    vmem = pl.BlockSpec(memory_space=pltpu.VMEM)
    embeddings, logprob = pl.pallas_call(
        whole_kernel,
        out_shape=(
            jax.ShapeDtypeStruct((OWN, 1024), BF16),
            jax.ShapeDtypeStruct((2, TOK_DEV // 2), F32),
        ),
        in_specs=[pl.BlockSpec(memory_space=pltpu.SMEM)] + [vmem] * 11,
        out_specs=(vmem, vmem),
        scratch_shapes=[
            pltpu.VMEM((GROUP, PACK, 256), BF16),
            pltpu.VMEM((GROUP, KMAX * CHAR_DIM, SLICE), BF16),
            pltpu.VMEM((GROUP, 8, SLICE), F32),
            pltpu.VMEM((8, 256, 128), BF16),
            pltpu.VMEM((BLOCK, 512), BF16),
            pltpu.VMEM((8, 256, WIDE), BF16),
            pltpu.VMEM((BLOCK, WIDE), F32),
            pltpu.VMEM((GROUP, BLOCK, WIDE), BF16),
            pltpu.VMEM((BLOCK, WIDE), BF16),
            pltpu.VMEM((CHUNKS, GROUP, OWN, WIDTH), BF16),
            pltpu.VMEM((CHUNKS, GROUP - 1, OWN, WIDTH), BF16),
            pltpu.VMEM((4, 16, 1024), BF16),
            pltpu.VMEM((2, TOK_DEV, 1024), BF16),
            pltpu.VMEM((2, CHUNKS, GROUP, OWN, WIDTH), BF16),
            pltpu.VMEM((2, BLOCK, 2 * TOK_DEV), F32),
            pltpu.VMEM((2, 4, 128), F32),
            pltpu.VMEM((16, 4, 128), F32),
            pltpu.VMEM((4, 4, 128), F32),
            pltpu.SemaphoreType.DMA((TOTAL,)),
            pltpu.SemaphoreType.DMA((TOTAL,)),
        ],
        compiler_params=pltpu.CompilerParams(
            collective_id=0, has_side_effects=True, vmem_limit_bytes=56 << 20
        ),
        name="whole",
    )(
        counts, char_ids, char_table.T, conv_weight, conv_bias.reshape(1, SLICE), highway_hid, highway_gate,
        hid_bias.reshape(1, SLICE), gate_bias.reshape(1, SLICE), proj_weight, hidden,
        targets.reshape(64, TOK_DEV // 2),
    )
    return embeddings, logprob.reshape(TOK_DEV)


def solution(mesh):
    return jax.shard_map(
        on_device,
        mesh=mesh,
        in_specs=(
            P(None, "tok"),
            P(),
            P(None, "word"),
            P("word"),
            P(None, "word"),
            P(None, "word"),
            P("word"),
            P("word"),
            P("word", None),
            P("tok", None),
            P(),
            P(),
        ),
        out_specs=(P(("tok", "word"), None), P("tok")),
        check_vma=False,
    )
```

```python
import functools

import jax
import jax.numpy as jnp
from jax import lax
from jax.experimental import pallas as pl
from jax.experimental.pallas import tpu as pltpu
from jax.sharding import PartitionSpec as P

CHAR_DIM = 16
KMAX = 7
CHAR_LEN = 24
FILTERS = 2048
TOK_DEV = 256
MESH = pl.DeviceIdType.MESH
BF16 = jnp.bfloat16
F32 = jnp.float32

GROUP = 4
OWN = 104
BLOCK = GROUP * OWN
SLICE = 128
WIDE = GROUP * SLICE
PACK = 2560
PIECE = PACK // 16
HALF = BLOCK // 2
CHUNKS = 2
WIDTH = 1024 // CHUNKS


def dot(a, b, contract=None, precision=None):
    if contract is None:
        return jnp.dot(a, b, preferred_element_type=F32, precision=precision)
    return lax.dot_general(a, b, (contract, ((), ())), preferred_element_type=F32)


def iota(shape, axis):
    return lax.broadcasted_iota(jnp.int32, shape, axis)


def one_hot(condition):
    return condition.astype(F32).astype(BF16)


COPIES = {
    "conv": 3, "bias": 3, "weight_z": 6, "weight_x": 12, "weight_far": 6, "weight_core": 6,
    "feats": 4, "feats_far": 2, "parts": 3 * CHUNKS, "row_z": 3, "row_zlo": 3, "row_y": 2, "row_far": 2,
    "emb_x": 3 * CHUNKS, "emb_core": 4 * CHUNKS, "stat_z": 15, "stat_y": 3,
}
FIRST, TOTAL = {}, 0
for name, amount in COPIES.items():
    FIRST[name] = TOTAL
    TOTAL += amount


def merge_stats(pieces):
    half = pieces[0].shape[0] // 2
    top = pieces[0][:half]
    for piece in pieces[1:]:
        top = jnp.maximum(top, piece[:half])
    total = sum(jnp.exp(piece[:half] - top) for piece in pieces)
    pick = sum(piece[half:] for piece in pieces)
    return jnp.concatenate([top + jnp.log(total), pick], axis=0)


def whole_kernel(
    counts_ref, ids_ref, table_ref, conv_ref, cbias_ref, hid_ref, gate_ref, hbias_ref, gbias_ref,
    proj_ref, hidden_ref, targets_ref,
    out_ref, logprob_ref,
    weights, convs, biases, tables, chars, shifted, best, feats, highway, parts, arrived,
    pieces, rows, words, scores, stat, zstat, ystat,
    send_sem, recv_sem,
):
    tok, word = lax.axis_index("tok"), lax.axis_index("word")
    zhi, x, core = tok // 8, (tok // 2) % 4, tok % 2
    y, zlo = word // 4, word % 4

    def at(zhi_to=zhi, x_to=x, core_to=core, y_to=y, zlo_to=zlo):
        return (zhi_to * 8 + x_to * 2 + core_to, y_to * 4 + zlo_to)

    sends = []

    def copy(name, index, src, dst, to):
        number = FIRST[name] + index
        return pltpu.make_async_remote_copy(
            src_ref=src, dst_ref=dst, send_sem=send_sem.at[number], recv_sem=recv_sem.at[number],
            device_id=to, device_id_type=MESH,
        )

    def start(name, index, src, dst, to):
        c = copy(name, index, src, dst, to)
        c.start()
        sends.append(c)

    def arrive(name, index, ref, to):
        copy(name, index, ref, ref, to).wait_recv()

    barrier = pltpu.get_barrier_semaphore()
    partners = [at(core_to=core ^ 1)]
    for d in (1, 2, 3):
        partners += [at(x_to=x ^ d), at(y_to=y ^ d)]
    partners += [at(zhi_to=zhi ^ (d >> 2), zlo_to=zlo ^ (d & 3)) for d in range(1, 16)]
    for partner in partners:
        pl.semaphore_signal(barrier, inc=1, device_id=partner, device_id_type=MESH)

    convs[zlo] = conv_ref[...]
    biases[zlo, 0:1, :] = cbias_ref[...]
    biases[zlo, 1:2, :] = hbias_ref[...]
    biases[zlo, 2:3, :] = gbias_ref[...]
    weights[zlo, 0:2048, 0:128] = hid_ref[...]
    weights[zlo, 0:2048, 128:256] = gate_ref[...]
    for cb in range(4):
        weights[zlo, 2048 + cb * 128 : 2176 + cb * 128, :] = proj_ref[:, cb * 256 : cb * 256 + 256]
    place = word * 16 + iota((16, TOK_DEV), 0)
    place = jnp.where(zhi >= 2, TOK_DEV - 1 - place, place)
    pieces[zhi] = dot(one_hot(place == iota((16, TOK_DEV), 1)), hidden_ref[...]).astype(BF16)

    row = iota((BLOCK, 1), 0)
    block = (row >= OWN).astype(jnp.int32) + (row >= 2 * OWN).astype(jnp.int32) + (row >= 3 * OWN).astype(jnp.int32)
    source = row + block * (BLOCK - OWN) + zlo * OWN
    chosen = one_hot(source == iota((BLOCK, GROUP * BLOCK), 1))
    spelled = dot(chosen, ids_ref[...].astype(F32).astype(BF16), ((1,), (1,))).astype(jnp.int32)
    letter = iota((BLOCK, 256), 1)
    for j in range(8):
        shift = one_hot(iota((CHAR_DIM, 128), 1) == iota((CHAR_DIM, 128), 0) + CHAR_DIM * j)
        tables[j] = dot(table_ref[...], shift, ((0,), (0,))).astype(BF16)
    for i in range(3):
        total = jnp.zeros((BLOCK, 128), F32)
        for j in range(8):
            p = 8 * i + j
            total += dot(one_hot(spelled[:, p : p + 1] == letter), tables[j])
        chars[:, 128 * i : 128 * i + 128] = total.astype(BF16)
    chars[:, 384:512] = jnp.zeros((BLOCK, 128), BF16)

    pl.semaphore_wait(barrier, len(partners))

    x_next, x_last, x_far = (x + 1) % 4, (x + 3) % 4, (x + 2) % 4
    y_next, y_last, y_far = (y + 1) % 4, (y + 3) % 4, (y + 2) % 4

    def piece(part, x_of):
        return pl.ds(pl.multiple_of(part * (PACK // 2) + core * (4 * PIECE) + x_of * PIECE, PIECE), PIECE)

    def core_pieces(part, core_of):
        return pl.ds(pl.multiple_of(part * (PACK // 2) + core_of * (4 * PIECE), 4 * PIECE), 4 * PIECE)

    def start_weights(part):
        for d in (1, 2, 3):
            ref = weights.at[zlo, piece(part, x)]
            start("weight_z", part * 3 + d - 1, ref, ref, at(zlo_to=zlo ^ d))

    for d in (1, 2, 3):
        to = at(zlo_to=zlo ^ d)
        start("conv", d - 1, convs.at[zlo], convs.at[zlo], to)
        start("bias", d - 1, biases.at[zlo], biases.at[zlo], to)
    start_weights(0)
    start_weights(1)
    for d in (1, 2, 3):
        start("row_z", d - 1, pieces.at[zhi], pieces.at[zhi], at(zhi_to=zhi ^ d))

    for d in (1, 2, 3):
        arrive("conv", d - 1, convs.at[zlo ^ d], at(zlo_to=zlo ^ d))
        arrive("bias", d - 1, biases.at[zlo ^ d], at(zlo_to=zlo ^ d))
    tap = iota((KMAX * CHAR_DIM, WIDE), 0) >> 4
    number = y * WIDE + iota((KMAX * CHAR_DIM, WIDE), 1)
    keep = tap < 1 + ((number * KMAX) >> 11)
    filters = jnp.concatenate([convs[q] for q in range(GROUP)], axis=1).astype(F32)
    filters = jnp.where(keep, filters, 0.0).astype(BF16)
    for j in range(8):
        shifted[j] = jnp.zeros((256, WIDE), BF16)
        shifted[j, CHAR_DIM * j : CHAR_DIM * (j + KMAX), :] = filters
    best[...] = jnp.full((BLOCK, WIDE), -3e38, F32)

    bias = jnp.concatenate([biases[q, 0:1, :] for q in range(GROUP)], axis=1)
    for h in range(2):
        low, high = h * HALF, h * HALF + HALF

        def conv_step(j, carry):
            taps = shifted[j]
            top = dot(chars[low:high, 0:256], taps)
            top = jnp.maximum(top, dot(chars[low:high, 128:384], taps))
            top = jnp.maximum(top, dot(chars[low:high, 256:512], taps))
            best[low:high, :] = jnp.maximum(best[low:high, :], top)
            return carry

        lax.fori_loop(0, 8, conv_step, 0)
        feats[y, low:high, :] = jnp.tanh(best[low:high, :] + bias).astype(BF16)
        ref = feats.at[y, low:high]
        start("feats", h, ref, ref, at(y_to=y_next))
        start("feats", 2 + h, ref, ref, at(y_to=y_last))

    def weights_to_x(part):
        for d in (1, 2, 3):
            ref = weights.at[zlo ^ d, piece(part, x)]
            arrive("weight_z", part * 3 + d - 1, ref, at(zlo_to=zlo ^ d))
            start("weight_x", part * 6 + d - 1, ref, ref, at(x_to=x_next))
            start("weight_x", part * 6 + 2 + d, ref, ref, at(x_to=x_last))

    def weights_far(part):
        neighbour, other, base = ((x_last, x_next, 0), (x_next, x_last, 9))[part]
        for d in (1, 2, 3):
            ref = weights.at[zlo ^ d, piece(part, neighbour)]
            arrive("weight_x", base + d - 1, ref, at(x_to=neighbour))
            start("weight_far", part * 3 + d - 1, ref, ref, at(x_to=other))

    def feats_far(h):
        neighbour, other = ((y_last, y_next), (y_next, y_last))[h]
        ref = feats.at[neighbour, h * HALF : h * HALF + HALF]
        arrive("feats", 3 * h, ref, at(y_to=neighbour))
        start("feats_far", h, ref, ref, at(y_to=other))

    weights_to_x(0)
    feats_far(0)
    weights_to_x(1)
    feats_far(1)

    own_rows = pl.ds(pl.multiple_of(word * 16, 16), 16)

    def y_rows(y_of):
        return pl.ds(pl.multiple_of(y_of * 64, 64), 64)

    for d in (1, 2, 3):
        arrive("row_z", d - 1, pieces.at[zhi ^ d], at(zhi_to=zhi ^ d))
    position = word * 16 + iota((16, 1024), 0)
    for a in range(2):
        lower = position < counts_ref[a * 8 + x * 2 + core]
        rows[a, own_rows, :] = jnp.where(
            lower, pieces[a].astype(F32), pieces[a + 2].astype(F32)
        ).astype(BF16)
    for d in (1, 2, 3):
        start("row_zlo", d - 1, rows.at[:, own_rows], rows.at[:, own_rows], at(zlo_to=zlo ^ d))

    weights_far(0)
    weights_far(1)

    flip = one_hot(iota((TOK_DEV, TOK_DEV), 0) + iota((TOK_DEV, TOK_DEV), 1) == TOK_DEV - 1)
    lane = iota((1, TOK_DEV), 1)

    def shard_targets(shard):
        both = targets_ref[pl.ds(2 * shard, 2), :]
        return jnp.concatenate([both[0:1, :], both[1:2, :]], axis=1)

    wanted = []
    for a in range(2):
        shard = a * 8 + x * 2 + core
        upper = shard_targets(shard + 16)
        high, low = upper >> 8, upper & 255
        high = dot(high.astype(F32).astype(BF16), flip).astype(jnp.int32)
        low = dot(low.astype(F32).astype(BF16), flip).astype(jnp.int32)
        target = jnp.where(lane < counts_ref[shard], shard_targets(shard), high * 256 + low)
        owner = target // (GROUP * BLOCK)
        rest = target - owner * (GROUP * BLOCK)
        slot = rest // OWN
        here = ((owner >> 3) == zhi) & (slot == word)
        local = ((owner & 1) ^ core) * BLOCK + ((owner >> 1) & 3) * OWN + rest - slot * OWN
        wanted.append(jnp.where(here, local, -1))
    wanted = jnp.concatenate(wanted, axis=1)

    for part, neighbour, base in ((0, x_next, 3), (1, x_last, 6)):
        for d in (1, 2, 3):
            q = zlo ^ d
            arrive("weight_x", base + d - 1, weights.at[q, piece(part, neighbour)], at(x_to=neighbour))
            arrive("weight_far", part * 3 + d - 1, weights.at[q, piece(part, x_far)], at(x_to=neighbour))
            ref = weights.at[q, core_pieces(part, core)]
            start("weight_core", part * 3 + d - 1, ref, ref, at(core_to=core ^ 1))
    for d in (1, 2, 3):
        theirs = pl.ds(pl.multiple_of(y * 64 + (zlo ^ d) * 16, 16), 16)
        arrive("row_zlo", d - 1, rows.at[:, theirs], at(zlo_to=zlo ^ d))
    ref = rows.at[:, y_rows(y)]
    start("row_y", 0, ref, ref, at(y_to=y_next))
    start("row_y", 1, ref, ref, at(y_to=y_last))

    arrive("feats", 1, feats.at[y_last, HALF:BLOCK], at(y_to=y_last))
    arrive("feats", 2, feats.at[y_next, 0:HALF], at(y_to=y_next))
    arrive("feats_far", 0, feats.at[y_far, 0:HALF], at(y_to=y_last))
    arrive("feats_far", 1, feats.at[y_far, HALF:BLOCK], at(y_to=y_next))

    for d in range(4):
        q = zlo ^ d
        if d:
            for part in range(2):
                ref = weights.at[q, core_pieces(part, core ^ 1)]
                arrive("weight_core", part * 3 + d - 1, ref, at(core_to=core ^ 1))
        mixed = dot(feats[0], weights[q, 0:512, :])
        for g in range(1, GROUP):
            mixed += dot(feats[g], weights[q, 512 * g : 512 * g + 512, :])
        hid_in = mixed[:, :128] + biases[q, 1:2, :]
        gate_in = mixed[:, 128:] + biases[q, 2:3, :]
        opened = jax.nn.sigmoid(gate_in)
        columns = pl.ds(pl.multiple_of(q * SLICE, SLICE), SLICE)
        carried = feats[y, :, columns].astype(F32)
        highway[:, columns] = (opened * jnp.maximum(hid_in, 0.0) + (1.0 - opened) * carried).astype(BF16)

    for c in range(CHUNKS):
        for cb in range(c * WIDTH // 256, (c + 1) * WIDTH // 256):
            matrix = jnp.concatenate(
                [weights[q, 2048 + cb * 128 : 2176 + cb * 128, :] for q in range(GROUP)], axis=0
            )
            product = dot(highway[...], matrix).astype(BF16)
            column = cb * 256 - c * WIDTH
            for g in range(GROUP):
                parts[c, g, :, column : column + 256] = product[g * OWN : g * OWN + OWN, :]
        for d in (1, 2, 3):
            start("parts", 3 * c + d - 1, parts.at[c, y ^ d], arrived.at[c, d - 1], at(y_to=y ^ d))

    arrive("row_y", 0, rows.at[:, y_rows(y_last)], at(y_to=y_last))
    ref = rows.at[0, y_rows(y_last)]
    start("row_far", 0, ref, ref, at(y_to=y_next))
    arrive("row_y", 1, rows.at[:, y_rows(y_next)], at(y_to=y_next))
    ref = rows.at[1, y_rows(y_next)]
    start("row_far", 1, ref, ref, at(y_to=y_last))

    def sum_chunk(c):
        total = parts[c, y].astype(F32)
        for d in (1, 2, 3):
            arrive("parts", 3 * c + d - 1, arrived.at[c, d - 1], at(y_to=y ^ d))
            total += arrived[c, d - 1].astype(F32)
        own_words = total.astype(BF16)
        out_ref[:, c * WIDTH : c * WIDTH + WIDTH] = own_words
        words[core, c, x] = own_words
        ref = words.at[core, c, x]
        for k in (2, 1, 3):
            start("emb_x", 3 * c + k - 1, ref, ref, at(x_to=x ^ k))
        start("emb_core", 4 * c, ref, ref, at(core_to=core ^ 1))

    def share_chunk(c):
        for k in (1, 3, 2):
            ref = words.at[core, c, x ^ k]
            arrive("emb_x", 3 * c + k - 1, ref, at(x_to=x ^ k))
            start("emb_core", 4 * c + k, ref, ref, at(core_to=core ^ 1))

    def score_side(c, side):
        queries = rows[:, :, c * WIDTH : c * WIDTH + WIDTH].reshape(2 * TOK_DEV, WIDTH)
        values = dot(words[core ^ side, c].reshape(BLOCK, WIDTH), queries, ((1,), (1,)))
        scores[side] = values if c == 0 else scores[side] + values

    found = []

    def statistics(side):
        values = scores[side]
        top = jnp.max(values, axis=0, keepdims=True)
        total = jnp.sum(jnp.exp(values - top), axis=0, keepdims=True)
        hits = iota((BLOCK, 2 * TOK_DEV), 0) == wanted - side * BLOCK
        pick = jnp.sum(jnp.where(hits, values, 0.0), axis=0, keepdims=True)
        return jnp.concatenate([top + jnp.log(total), pick], axis=0)

    def score_chunk(c):
        if c == 0:
            arrive("row_far", 0, rows.at[0, y_rows(y_far)], at(y_to=y_last))
            arrive("row_far", 1, rows.at[1, y_rows(y_far)], at(y_to=y_next))
        score_side(c, 0)
        if c == CHUNKS - 1:
            found.append(statistics(0))
        for k in range(4):
            arrive("emb_core", 4 * c + k, words.at[core ^ 1, c, x ^ k], at(core_to=core ^ 1))
        score_side(c, 1)

    for step in range(CHUNKS + 2):
        for lag, action in ((0, sum_chunk), (2, score_chunk), (1, share_chunk)):
            if 0 <= step - lag < CHUNKS:
                action(step - lag)

    both = merge_stats([found[0], statistics(1)])
    for a in range(2):
        for r in range(2):
            first = a * TOK_DEV + r * 128
            stat[a, r : r + 1, :] = both[0:1, first : first + 128]
            stat[a, r + 2 : r + 3, :] = both[1:2, first : first + 128]
    for d in range(1, 16):
        z_to = zhi ^ (d >> 2)
        start(
            "stat_z", d - 1, stat.at[z_to % 2], zstat.at[zhi * 4 + zlo],
            at(zhi_to=z_to, zlo_to=zlo ^ (d & 3)),
        )
    zstat[zhi * 4 + zlo] = stat[zhi % 2]
    for d in range(1, 16):
        z_of, l_of = zhi ^ (d >> 2), zlo ^ (d & 3)
        arrive("stat_z", d - 1, zstat.at[z_of * 4 + l_of], at(zhi_to=z_of, zlo_to=l_of))
    ystat[y] = merge_stats([zstat[n] for n in range(16)])
    for d in (1, 2, 3):
        start("stat_y", d - 1, ystat.at[y], ystat.at[y], at(y_to=y ^ d))
    for d in (1, 2, 3):
        arrive("stat_y", d - 1, ystat.at[y ^ d], at(y_to=y ^ d))
    both = merge_stats([ystat[n] for n in range(4)])
    result = both[2:4] - both[0:2]
    result = jnp.concatenate([result[0:1], result[1:2]], axis=1)
    first = result.astype(BF16)
    left = result - first.astype(F32)
    second = left.astype(BF16)
    third = (left - second.astype(F32)).astype(BF16)
    turned = dot(first, flip) + dot(second, flip) + dot(third, flip)
    result = jnp.where(zhi >= 2, turned, result)
    result = jnp.where(lane < counts_ref[tok], result, 0.0)
    logprob_ref[0:1, :] = result[:, 0:128]
    logprob_ref[1:2, :] = result[:, 128:256]
    for c in sends:
        c.wait_send()


def on_device(
    char_ids,
    char_table,
    conv_weight,
    conv_bias,
    highway_hid,
    highway_gate,
    hid_bias,
    gate_bias,
    proj_weight,
    hidden,
    targets,
    counts,
):
    vmem = pl.BlockSpec(memory_space=pltpu.VMEM)
    embeddings, logprob = pl.pallas_call(
        whole_kernel,
        out_shape=(
            jax.ShapeDtypeStruct((OWN, 1024), BF16),
            jax.ShapeDtypeStruct((2, TOK_DEV // 2), F32),
        ),
        in_specs=[pl.BlockSpec(memory_space=pltpu.SMEM)] + [vmem] * 11,
        out_specs=(vmem, vmem),
        scratch_shapes=[
            pltpu.VMEM((GROUP, PACK, 256), BF16),
            pltpu.VMEM((GROUP, KMAX * CHAR_DIM, SLICE), BF16),
            pltpu.VMEM((GROUP, 8, SLICE), F32),
            pltpu.VMEM((8, 256, 128), BF16),
            pltpu.VMEM((BLOCK, 512), BF16),
            pltpu.VMEM((8, 256, WIDE), BF16),
            pltpu.VMEM((BLOCK, WIDE), F32),
            pltpu.VMEM((GROUP, BLOCK, WIDE), BF16),
            pltpu.VMEM((BLOCK, WIDE), BF16),
            pltpu.VMEM((CHUNKS, GROUP, OWN, WIDTH), BF16),
            pltpu.VMEM((CHUNKS, GROUP - 1, OWN, WIDTH), BF16),
            pltpu.VMEM((4, 16, 1024), BF16),
            pltpu.VMEM((2, TOK_DEV, 1024), BF16),
            pltpu.VMEM((2, CHUNKS, GROUP, OWN, WIDTH), BF16),
            pltpu.VMEM((2, BLOCK, 2 * TOK_DEV), F32),
            pltpu.VMEM((2, 4, 128), F32),
            pltpu.VMEM((16, 4, 128), F32),
            pltpu.VMEM((4, 4, 128), F32),
            pltpu.SemaphoreType.DMA((TOTAL,)),
            pltpu.SemaphoreType.DMA((TOTAL,)),
        ],
        compiler_params=pltpu.CompilerParams(
            collective_id=0, has_side_effects=True, vmem_limit_bytes=56 << 20
        ),
        name="whole",
    )(
        counts, char_ids, char_table.T, conv_weight, conv_bias.reshape(1, SLICE), highway_hid, highway_gate,
        hid_bias.reshape(1, SLICE), gate_bias.reshape(1, SLICE), proj_weight, hidden,
        targets.reshape(64, TOK_DEV // 2),
    )
    return embeddings, logprob.reshape(TOK_DEV)


def solution(mesh):
    return jax.shard_map(
        on_device,
        mesh=mesh,
        in_specs=(
            P(None, "tok"),
            P(),
            P(None, "word"),
            P("word"),
            P(None, "word"),
            P(None, "word"),
            P("word"),
            P("word"),
            P("word", None),
            P("tok", None),
            P(),
            P(),
        ),
        out_specs=(P(("tok", "word"), None), P("tok")),
        check_vma=False,
    )
```

```python
import functools

import jax
import jax.numpy as jnp
from jax import lax
from jax.experimental import pallas as pl
from jax.experimental.pallas import tpu as pltpu
from jax.sharding import PartitionSpec as P

CHAR_DIM = 16
KMAX = 7
CHAR_LEN = 24
FILTERS = 2048
TOK_DEV = 256
MESH = pl.DeviceIdType.MESH
BF16 = jnp.bfloat16
F32 = jnp.float32

GROUP = 4
OWN = 104
BLOCK = GROUP * OWN
SLICE = 128
WIDE = GROUP * SLICE
PACK = 2560
PIECE = PACK // 16
HALF = BLOCK // 2
CHUNKS = 2
WIDTH = 1024 // CHUNKS


def dot(a, b, contract=None, precision=None):
    if contract is None:
        return jnp.dot(a, b, preferred_element_type=F32, precision=precision)
    return lax.dot_general(a, b, (contract, ((), ())), preferred_element_type=F32)


def iota(shape, axis):
    return lax.broadcasted_iota(jnp.int32, shape, axis)


def one_hot(condition):
    return condition.astype(F32).astype(BF16)


COPIES = {
    "conv": 3, "bias": 3, "weight_z": 6, "weight_x": 12, "weight_far": 6, "weight_core": 6,
    "feats": 4, "feats_far": 2, "parts": 3 * CHUNKS, "row_z": 3, "row_zlo": 3, "row_y": 2, "row_far": 2,
    "emb_x": 3 * CHUNKS, "emb_core": 4 * CHUNKS, "stat_z": 15, "stat_y": 3,
}
FAR_FIRST = (8, 9, 10, 11, 4, 5, 6, 7, 12, 13, 14, 15, 3, 2, 1)
FIRST, TOTAL = {}, 0
for name, amount in COPIES.items():
    FIRST[name] = TOTAL
    TOTAL += amount


def merge_stats(pieces):
    half = pieces[0].shape[0] // 2
    top = pieces[0][:half]
    for piece in pieces[1:]:
        top = jnp.maximum(top, piece[:half])
    total = sum(jnp.exp(piece[:half] - top) for piece in pieces)
    pick = sum(piece[half:] for piece in pieces)
    return jnp.concatenate([top + jnp.log(total), pick], axis=0)


def whole_kernel(
    counts_ref, ids_ref, table_ref, conv_ref, cbias_ref, hid_ref, gate_ref, hbias_ref, gbias_ref,
    proj_ref, hidden_ref, targets_ref,
    out_ref, logprob_ref,
    weights, convs, biases, tables, chars, shifted, best, feats, highway, parts, arrived,
    pieces, rows, words, scores, stat, zstat, ystat,
    send_sem, recv_sem,
):
    tok, word = lax.axis_index("tok"), lax.axis_index("word")
    zhi, x, core = tok // 8, (tok // 2) % 4, tok % 2
    y, zlo = word // 4, word % 4

    def at(zhi_to=zhi, x_to=x, core_to=core, y_to=y, zlo_to=zlo):
        return (zhi_to * 8 + x_to * 2 + core_to, y_to * 4 + zlo_to)

    sends = []

    def copy(name, index, src, dst, to):
        number = FIRST[name] + index
        return pltpu.make_async_remote_copy(
            src_ref=src, dst_ref=dst, send_sem=send_sem.at[number], recv_sem=recv_sem.at[number],
            device_id=to, device_id_type=MESH,
        )

    def start(name, index, src, dst, to):
        c = copy(name, index, src, dst, to)
        c.start()
        sends.append(c)

    def arrive(name, index, ref, to):
        copy(name, index, ref, ref, to).wait_recv()

    barrier = pltpu.get_barrier_semaphore()
    partners = [at(zhi_to=zhi ^ (d >> 2), zlo_to=zlo ^ (d & 3)) for d in FAR_FIRST]
    for d in (2, 1, 3):
        partners += [at(x_to=x ^ d), at(y_to=y ^ d)]
    partners.append(at(core_to=core ^ 1))
    for partner in partners:
        pl.semaphore_signal(barrier, inc=1, device_id=partner, device_id_type=MESH)

    convs[zlo] = conv_ref[...]
    biases[zlo, 0:1, :] = cbias_ref[...]
    biases[zlo, 1:2, :] = hbias_ref[...]
    biases[zlo, 2:3, :] = gbias_ref[...]
    weights[zlo, 0:2048, 0:128] = hid_ref[...]
    weights[zlo, 0:2048, 128:256] = gate_ref[...]
    for cb in range(4):
        weights[zlo, 2048 + cb * 128 : 2176 + cb * 128, :] = proj_ref[:, cb * 256 : cb * 256 + 256]
    place = word * 16 + iota((16, TOK_DEV), 0)
    place = jnp.where(zhi >= 2, TOK_DEV - 1 - place, place)
    pieces[zhi] = dot(one_hot(place == iota((16, TOK_DEV), 1)), hidden_ref[...]).astype(BF16)

    row = iota((BLOCK, 1), 0)
    block = (row >= OWN).astype(jnp.int32) + (row >= 2 * OWN).astype(jnp.int32) + (row >= 3 * OWN).astype(jnp.int32)
    source = row + block * (BLOCK - OWN) + zlo * OWN
    chosen = one_hot(source == iota((BLOCK, GROUP * BLOCK), 1))
    spelled = dot(chosen, ids_ref[...].astype(F32).astype(BF16), ((1,), (1,))).astype(jnp.int32)
    letter = iota((BLOCK, 256), 1)
    for j in range(8):
        shift = one_hot(iota((CHAR_DIM, 128), 1) == iota((CHAR_DIM, 128), 0) + CHAR_DIM * j)
        tables[j] = dot(table_ref[...], shift, ((0,), (0,))).astype(BF16)
    for i in range(3):
        total = jnp.zeros((BLOCK, 128), F32)
        for j in range(8):
            p = 8 * i + j
            total += dot(one_hot(spelled[:, p : p + 1] == letter), tables[j])
        chars[:, 128 * i : 128 * i + 128] = total.astype(BF16)
    chars[:, 384:512] = jnp.zeros((BLOCK, 128), BF16)

    pl.semaphore_wait(barrier, len(partners))

    x_next, x_last, x_far = (x + 1) % 4, (x + 3) % 4, (x + 2) % 4
    y_next, y_last, y_far = (y + 1) % 4, (y + 3) % 4, (y + 2) % 4

    def piece(part, x_of):
        return pl.ds(pl.multiple_of(part * (PACK // 2) + core * (4 * PIECE) + x_of * PIECE, PIECE), PIECE)

    def core_pieces(part, core_of):
        return pl.ds(pl.multiple_of(part * (PACK // 2) + core_of * (4 * PIECE), 4 * PIECE), 4 * PIECE)

    def start_weights(part):
        for d in (1, 2, 3):
            ref = weights.at[zlo, piece(part, x)]
            start("weight_z", part * 3 + d - 1, ref, ref, at(zlo_to=zlo ^ d))

    for d in (1, 2, 3):
        to = at(zlo_to=zlo ^ d)
        start("conv", d - 1, convs.at[zlo], convs.at[zlo], to)
        start("bias", d - 1, biases.at[zlo], biases.at[zlo], to)
    start_weights(0)
    start_weights(1)
    for d in (2, 1, 3):
        start("row_z", d - 1, pieces.at[zhi], pieces.at[zhi], at(zhi_to=zhi ^ d))

    for d in (1, 2, 3):
        arrive("conv", d - 1, convs.at[zlo ^ d], at(zlo_to=zlo ^ d))
        arrive("bias", d - 1, biases.at[zlo ^ d], at(zlo_to=zlo ^ d))
    tap = iota((KMAX * CHAR_DIM, WIDE), 0) >> 4
    number = y * WIDE + iota((KMAX * CHAR_DIM, WIDE), 1)
    keep = tap < 1 + ((number * KMAX) >> 11)
    filters = jnp.concatenate([convs[q] for q in range(GROUP)], axis=1).astype(F32)
    filters = jnp.where(keep, filters, 0.0).astype(BF16)
    for j in range(8):
        shifted[j] = jnp.zeros((256, WIDE), BF16)
        shifted[j, CHAR_DIM * j : CHAR_DIM * (j + KMAX), :] = filters
    best[...] = jnp.full((BLOCK, WIDE), -3e38, F32)

    bias = jnp.concatenate([biases[q, 0:1, :] for q in range(GROUP)], axis=1)
    for h in range(2):
        low, high = h * HALF, h * HALF + HALF

        def conv_step(j, carry):
            taps = shifted[j]
            top = dot(chars[low:high, 0:256], taps)
            top = jnp.maximum(top, dot(chars[low:high, 128:384], taps))
            top = jnp.maximum(top, dot(chars[low:high, 256:512], taps))
            best[low:high, :] = jnp.maximum(best[low:high, :], top)
            return carry

        lax.fori_loop(0, 8, conv_step, 0)
        feats[y, low:high, :] = jnp.tanh(best[low:high, :] + bias).astype(BF16)
        ref = feats.at[y, low:high]
        start("feats", h, ref, ref, at(y_to=y_next))
        start("feats", 2 + h, ref, ref, at(y_to=y_last))

    def weights_to_x(part):
        for d in (1, 2, 3):
            ref = weights.at[zlo ^ d, piece(part, x)]
            arrive("weight_z", part * 3 + d - 1, ref, at(zlo_to=zlo ^ d))
            start("weight_x", part * 6 + d - 1, ref, ref, at(x_to=x_next))
            start("weight_x", part * 6 + 2 + d, ref, ref, at(x_to=x_last))

    def weights_far(part):
        neighbour, other, base = ((x_last, x_next, 0), (x_next, x_last, 9))[part]
        for d in (1, 2, 3):
            ref = weights.at[zlo ^ d, piece(part, neighbour)]
            arrive("weight_x", base + d - 1, ref, at(x_to=neighbour))
            start("weight_far", part * 3 + d - 1, ref, ref, at(x_to=other))

    def feats_far(h):
        neighbour, other = ((y_last, y_next), (y_next, y_last))[h]
        ref = feats.at[neighbour, h * HALF : h * HALF + HALF]
        arrive("feats", 3 * h, ref, at(y_to=neighbour))
        start("feats_far", h, ref, ref, at(y_to=other))

    weights_to_x(0)
    feats_far(0)
    weights_to_x(1)
    feats_far(1)

    own_rows = pl.ds(pl.multiple_of(word * 16, 16), 16)

    def y_rows(y_of):
        return pl.ds(pl.multiple_of(y_of * 64, 64), 64)

    for d in (1, 2, 3):
        arrive("row_z", d - 1, pieces.at[zhi ^ d], at(zhi_to=zhi ^ d))
    position = word * 16 + iota((16, 1024), 0)
    for a in range(2):
        lower = position < counts_ref[a * 8 + x * 2 + core]
        rows[a, own_rows, :] = jnp.where(
            lower, pieces[a].astype(F32), pieces[a + 2].astype(F32)
        ).astype(BF16)
    for d in (1, 2, 3):
        start("row_zlo", d - 1, rows.at[:, own_rows], rows.at[:, own_rows], at(zlo_to=zlo ^ d))

    weights_far(0)
    weights_far(1)

    flip = one_hot(iota((TOK_DEV, TOK_DEV), 0) + iota((TOK_DEV, TOK_DEV), 1) == TOK_DEV - 1)
    lane = iota((1, TOK_DEV), 1)

    def shard_targets(shard):
        both = targets_ref[pl.ds(2 * shard, 2), :]
        return jnp.concatenate([both[0:1, :], both[1:2, :]], axis=1)

    wanted = []
    for a in range(2):
        shard = a * 8 + x * 2 + core
        upper = shard_targets(shard + 16)
        high, low = upper >> 8, upper & 255
        high = dot(high.astype(F32).astype(BF16), flip).astype(jnp.int32)
        low = dot(low.astype(F32).astype(BF16), flip).astype(jnp.int32)
        target = jnp.where(lane < counts_ref[shard], shard_targets(shard), high * 256 + low)
        owner = target // (GROUP * BLOCK)
        rest = target - owner * (GROUP * BLOCK)
        slot = rest // OWN
        here = ((owner >> 3) == zhi) & (slot == word)
        local = ((owner & 1) ^ core) * BLOCK + ((owner >> 1) & 3) * OWN + rest - slot * OWN
        wanted.append(jnp.where(here, local, -1))
    wanted = jnp.concatenate(wanted, axis=1)

    for part, neighbour, base in ((0, x_next, 3), (1, x_last, 6)):
        for d in (1, 2, 3):
            q = zlo ^ d
            arrive("weight_x", base + d - 1, weights.at[q, piece(part, neighbour)], at(x_to=neighbour))
            arrive("weight_far", part * 3 + d - 1, weights.at[q, piece(part, x_far)], at(x_to=neighbour))
            ref = weights.at[q, core_pieces(part, core)]
            start("weight_core", part * 3 + d - 1, ref, ref, at(core_to=core ^ 1))
    for d in (1, 2, 3):
        theirs = pl.ds(pl.multiple_of(y * 64 + (zlo ^ d) * 16, 16), 16)
        arrive("row_zlo", d - 1, rows.at[:, theirs], at(zlo_to=zlo ^ d))
    ref = rows.at[:, y_rows(y)]
    start("row_y", 0, ref, ref, at(y_to=y_next))
    start("row_y", 1, ref, ref, at(y_to=y_last))

    arrive("feats", 1, feats.at[y_last, HALF:BLOCK], at(y_to=y_last))
    arrive("feats", 2, feats.at[y_next, 0:HALF], at(y_to=y_next))
    arrive("feats_far", 0, feats.at[y_far, 0:HALF], at(y_to=y_last))
    arrive("feats_far", 1, feats.at[y_far, HALF:BLOCK], at(y_to=y_next))

    for d in range(4):
        q = zlo ^ d
        if d:
            for part in range(2):
                ref = weights.at[q, core_pieces(part, core ^ 1)]
                arrive("weight_core", part * 3 + d - 1, ref, at(core_to=core ^ 1))
        mixed = dot(feats[0], weights[q, 0:512, :])
        for g in range(1, GROUP):
            mixed += dot(feats[g], weights[q, 512 * g : 512 * g + 512, :])
        hid_in = mixed[:, :128] + biases[q, 1:2, :]
        gate_in = mixed[:, 128:] + biases[q, 2:3, :]
        opened = jax.nn.sigmoid(gate_in)
        columns = pl.ds(pl.multiple_of(q * SLICE, SLICE), SLICE)
        carried = feats[y, :, columns].astype(F32)
        highway[:, columns] = (opened * jnp.maximum(hid_in, 0.0) + (1.0 - opened) * carried).astype(BF16)

    for c in range(CHUNKS):
        for cb in range(c * WIDTH // 256, (c + 1) * WIDTH // 256):
            matrix = jnp.concatenate(
                [weights[q, 2048 + cb * 128 : 2176 + cb * 128, :] for q in range(GROUP)], axis=0
            )
            product = dot(highway[...], matrix).astype(BF16)
            column = cb * 256 - c * WIDTH
            for g in range(GROUP):
                parts[c, g, :, column : column + 256] = product[g * OWN : g * OWN + OWN, :]
        for d in (2, 1, 3):
            start("parts", 3 * c + d - 1, parts.at[c, y ^ d], arrived.at[c, d - 1], at(y_to=y ^ d))

    arrive("row_y", 0, rows.at[:, y_rows(y_last)], at(y_to=y_last))
    ref = rows.at[0, y_rows(y_last)]
    start("row_far", 0, ref, ref, at(y_to=y_next))
    arrive("row_y", 1, rows.at[:, y_rows(y_next)], at(y_to=y_next))
    ref = rows.at[1, y_rows(y_next)]
    start("row_far", 1, ref, ref, at(y_to=y_last))

    def sum_chunk(c):
        total = parts[c, y].astype(F32)
        for d in (1, 2, 3):
            arrive("parts", 3 * c + d - 1, arrived.at[c, d - 1], at(y_to=y ^ d))
            total += arrived[c, d - 1].astype(F32)
        own_words = total.astype(BF16)
        out_ref[:, c * WIDTH : c * WIDTH + WIDTH] = own_words
        words[core, c, x] = own_words
        ref = words.at[core, c, x]
        for k in (2, 1, 3):
            start("emb_x", 3 * c + k - 1, ref, ref, at(x_to=x ^ k))
        start("emb_core", 4 * c, ref, ref, at(core_to=core ^ 1))

    def share_chunk(c):
        for k in (1, 3, 2):
            ref = words.at[core, c, x ^ k]
            arrive("emb_x", 3 * c + k - 1, ref, at(x_to=x ^ k))
            start("emb_core", 4 * c + k, ref, ref, at(core_to=core ^ 1))

    def score_side(c, side):
        queries = rows[:, :, c * WIDTH : c * WIDTH + WIDTH].reshape(2 * TOK_DEV, WIDTH)
        values = dot(words[core ^ side, c].reshape(BLOCK, WIDTH), queries, ((1,), (1,)))
        scores[side] = values if c == 0 else scores[side] + values

    found = []

    def statistics(side):
        values = scores[side]
        top = jnp.max(values, axis=0, keepdims=True)
        total = jnp.sum(jnp.exp(values - top), axis=0, keepdims=True)
        hits = iota((BLOCK, 2 * TOK_DEV), 0) == wanted - side * BLOCK
        pick = jnp.sum(jnp.where(hits, values, 0.0), axis=0, keepdims=True)
        return jnp.concatenate([top + jnp.log(total), pick], axis=0)

    def score_chunk(c):
        if c == 0:
            arrive("row_far", 0, rows.at[0, y_rows(y_far)], at(y_to=y_last))
            arrive("row_far", 1, rows.at[1, y_rows(y_far)], at(y_to=y_next))
        score_side(c, 0)
        if c == CHUNKS - 1:
            found.append(statistics(0))
        for k in range(4):
            arrive("emb_core", 4 * c + k, words.at[core ^ 1, c, x ^ k], at(core_to=core ^ 1))
        score_side(c, 1)

    for step in range(CHUNKS + 2):
        for lag, action in ((0, sum_chunk), (2, score_chunk), (1, share_chunk)):
            if 0 <= step - lag < CHUNKS:
                action(step - lag)

    both = merge_stats([found[0], statistics(1)])
    for a in range(2):
        for r in range(2):
            first = a * TOK_DEV + r * 128
            stat[a, r : r + 1, :] = both[0:1, first : first + 128]
            stat[a, r + 2 : r + 3, :] = both[1:2, first : first + 128]
    for d in FAR_FIRST:
        z_to = zhi ^ (d >> 2)
        start(
            "stat_z", d - 1, stat.at[z_to % 2], zstat.at[zhi * 4 + zlo],
            at(zhi_to=z_to, zlo_to=zlo ^ (d & 3)),
        )
    zstat[zhi * 4 + zlo] = stat[zhi % 2]
    for d in range(1, 16):
        z_of, l_of = zhi ^ (d >> 2), zlo ^ (d & 3)
        arrive("stat_z", d - 1, zstat.at[z_of * 4 + l_of], at(zhi_to=z_of, zlo_to=l_of))
    ystat[y] = merge_stats([zstat[n] for n in range(16)])
    for d in (2, 1, 3):
        start("stat_y", d - 1, ystat.at[y], ystat.at[y], at(y_to=y ^ d))
    for d in (1, 2, 3):
        arrive("stat_y", d - 1, ystat.at[y ^ d], at(y_to=y ^ d))
    both = merge_stats([ystat[n] for n in range(4)])
    result = both[2:4] - both[0:2]
    result = jnp.concatenate([result[0:1], result[1:2]], axis=1)
    first = result.astype(BF16)
    left = result - first.astype(F32)
    second = left.astype(BF16)
    third = (left - second.astype(F32)).astype(BF16)
    turned = dot(first, flip) + dot(second, flip) + dot(third, flip)
    result = jnp.where(zhi >= 2, turned, result)
    result = jnp.where(lane < counts_ref[tok], result, 0.0)
    logprob_ref[0:1, :] = result[:, 0:128]
    logprob_ref[1:2, :] = result[:, 128:256]
    for c in sends:
        c.wait_send()


def on_device(
    char_ids,
    char_table,
    conv_weight,
    conv_bias,
    highway_hid,
    highway_gate,
    hid_bias,
    gate_bias,
    proj_weight,
    hidden,
    targets,
    counts,
):
    vmem = pl.BlockSpec(memory_space=pltpu.VMEM)
    embeddings, logprob = pl.pallas_call(
        whole_kernel,
        out_shape=(
            jax.ShapeDtypeStruct((OWN, 1024), BF16),
            jax.ShapeDtypeStruct((2, TOK_DEV // 2), F32),
        ),
        in_specs=[pl.BlockSpec(memory_space=pltpu.SMEM)] + [vmem] * 11,
        out_specs=(vmem, vmem),
        scratch_shapes=[
            pltpu.VMEM((GROUP, PACK, 256), BF16),
            pltpu.VMEM((GROUP, KMAX * CHAR_DIM, SLICE), BF16),
            pltpu.VMEM((GROUP, 8, SLICE), F32),
            pltpu.VMEM((8, 256, 128), BF16),
            pltpu.VMEM((BLOCK, 512), BF16),
            pltpu.VMEM((8, 256, WIDE), BF16),
            pltpu.VMEM((BLOCK, WIDE), F32),
            pltpu.VMEM((GROUP, BLOCK, WIDE), BF16),
            pltpu.VMEM((BLOCK, WIDE), BF16),
            pltpu.VMEM((CHUNKS, GROUP, OWN, WIDTH), BF16),
            pltpu.VMEM((CHUNKS, GROUP - 1, OWN, WIDTH), BF16),
            pltpu.VMEM((4, 16, 1024), BF16),
            pltpu.VMEM((2, TOK_DEV, 1024), BF16),
            pltpu.VMEM((2, CHUNKS, GROUP, OWN, WIDTH), BF16),
            pltpu.VMEM((2, BLOCK, 2 * TOK_DEV), F32),
            pltpu.VMEM((2, 4, 128), F32),
            pltpu.VMEM((16, 4, 128), F32),
            pltpu.VMEM((4, 4, 128), F32),
            pltpu.SemaphoreType.DMA((TOTAL,)),
            pltpu.SemaphoreType.DMA((TOTAL,)),
        ],
        compiler_params=pltpu.CompilerParams(
            collective_id=0, has_side_effects=True, vmem_limit_bytes=56 << 20
        ),
        name="whole",
    )(
        counts, char_ids, char_table.T, conv_weight, conv_bias.reshape(1, SLICE), highway_hid, highway_gate,
        hid_bias.reshape(1, SLICE), gate_bias.reshape(1, SLICE), proj_weight, hidden,
        targets.reshape(64, TOK_DEV // 2),
    )
    return embeddings, logprob.reshape(TOK_DEV)


def solution(mesh):
    return jax.shard_map(
        on_device,
        mesh=mesh,
        in_specs=(
            P(None, "tok"),
            P(),
            P(None, "word"),
            P("word"),
            P(None, "word"),
            P(None, "word"),
            P("word"),
            P("word"),
            P("word", None),
            P("tok", None),
            P(),
            P(),
        ),
        out_specs=(P(("tok", "word"), None), P("tok")),
        check_vma=False,
    )
```
